512 devices in a mesh: seq: 32 (over z, core), head: 16 (over x, y).
Axes of the slice: x: 4, y: 4, z: 16, core: 2. Of those that a mesh axis runs over, the one named last changes fastest.
Arguments:
- queries: bfloat16 [4096, 16384], P('seq', 'head'), may hold values from -360 to 360, as said below
- keys: bfloat16 [4096, 1024], P('seq', 'head'), may hold values from -6 to 6
- values: bfloat16 [4096, 1024], P('seq', 'head'), may hold values from -6 to 6
- directions: bfloat16 [4096, 1024], P('seq', 'head'), may hold values from -6 to 6
- beta: float32 [4096, 8], P('seq'), may hold values from 0.25 to 2
- gain: float32 [128], replicated, may hold values from 0.25 to 1.75
Outputs:
- attended: bfloat16 [4096, 16384], P('seq', 'head')
The draws below stay inside these ranges and needn't reach their ends.
Inputs may be any that keep to these rules, and one draw needn't show every extreme that they name: `queries`: queries of order one; some rows may be far larger.
All inputs are finite; a program needn't handle non-finite values.
Results may differ from the reference program's by a relative error of at most 0.04.
Values may be sent and summed in bfloat16 or wider, within the bound.
A program may use at most 64 MiB of HBM per device.

```python
import jax
import jax.numpy as jnp
from jax import lax

HD = 128
GROUP_HEADS = 16
HEADS = 128
GROUPS = 8
TOK_DEV = 128
TOKENS = 4096
N_SEQ = 32


def draw_queries(key, part):
    samples = jnp.clip(jax.random.normal(key, (TOKENS, HEADS * HD), jnp.float32), -6.0, 6.0)
    return samples.astype(jnp.bfloat16)


def draw_beta(key, part):
    common = jax.random.uniform(jax.random.fold_in(key, 11), (TOKENS, GROUPS), jnp.float32, 1.95, 2.0)
    strong = jax.random.uniform(jax.random.fold_in(key, 12), (TOKENS, GROUPS), jnp.float32, 0.25, 2.0)
    picker = jax.random.randint(jax.random.fold_in(key, 13), (TOKENS, GROUPS), 0, 32)
    return jnp.where(picker == 0, strong, common).astype(jnp.float32)


def levels(rng, dims, split, least, top_value):
    def one(position, blocks):
        heights = jax.random.uniform(jax.random.fold_in(jax.random.fold_in(rng, 6), position), (blocks,), jnp.float32, least / len(split), top_value / len(split))
        return jnp.repeat(jnp.exp(heights), dims[position] // blocks).reshape((-1,) + (1,) * (len(dims) - position - 1))

    loudness = one(*split[0])
    for cut in split[1:]:
        loudness = loudness * one(*cut)
    return loudness


def bell_draw(stream_key, dims, scale, reach, cuts=(), kind=jnp.bfloat16):
    result = scale * jax.random.normal(stream_key, dims, jnp.float32)
    if cuts:
        result = result * levels(stream_key, dims, cuts, -0.22, 0.18)
    return jnp.clip(result, -reach, reach).astype(kind)


def setup_inputs(seed: int = 0) -> dict:
    key_of = jax.random.split(jax.random.key(seed), 7)
    queries = draw_queries(jax.random.fold_in(key_of[6], 71), 0)
    keys = bell_draw(key_of[1], (TOKENS, GROUPS * HD), 1.0, 6.0, ((0, 32), (1, 16)))
    values = bell_draw(key_of[2], (TOKENS, GROUPS * HD), 1.0, 6.0, ((0, 32), (1, 16)))
    directions = bell_draw(key_of[3], (TOKENS, GROUPS * HD), 1.0, 6.0, ((0, 32), (1, 16)))
    beta = draw_beta(jax.random.fold_in(key_of[6], 71), 0)
    gain = jnp.clip(1.0 + 0.15 * jax.random.normal(key_of[5], (HD,), jnp.float32), 0.25, 1.75)
    return {"queries": queries, "keys": keys, "values": values, "directions": directions, "beta": beta, "gain": gain}


exact_mode = lax.Precision.HIGHEST

def segment_terms(queries, keys, directions, beta):
    length, head_count, head_width = queries.shape
    raw_dirs = directions.astype(jnp.float32)
    unit_dirs = raw_dirs * lax.rsqrt(lax.optimization_barrier(jnp.sum(raw_dirs * raw_dirs, axis=1, keepdims=True)) + 1e-06)
    positions = jnp.arange(length)
    strict_mask = positions[:, None] > positions[None, :]
    causal_mask = positions[:, None] >= positions[None, :]
    intersections = jnp.where(strict_mask, jnp.dot(unit_dirs, unit_dirs.T, precision=exact_mode), 0.0)
    identity = jnp.eye(length, dtype=jnp.float32)
    scaled_dirs = beta[:, None] * unit_dirs
    keys_wide = keys.astype(jnp.float32)
    key_reach = jnp.where(strict_mask, jnp.dot(unit_dirs, keys_wide.T, precision=exact_mode), 0.0)
    solution = jax.scipy.linalg.solve_triangular(identity + intersections * beta[None, :], jnp.concatenate([key_reach, unit_dirs], axis=1), lower=True, unit_diagonal=True)
    moved_keys = keys_wide - jnp.dot(solution[:, :length].T, scaled_dirs, precision=exact_mode)
    transform = jnp.eye(head_width, dtype=jnp.float32) - jnp.dot(unit_dirs.T, beta[:, None] * solution[:, length:], precision=exact_mode)
    queries_wide = queries.astype(jnp.float32)
    query_reach = jnp.einsum('te,ihe->thi', unit_dirs, queries_wide, precision=exact_mode)
    query_reach = jnp.where(causal_mask.T[:, None, :], query_reach, 0.0)
    coefficients = jax.scipy.linalg.solve_triangular(identity + beta[:, None] * intersections, query_reach.reshape(length, head_count * length), lower=True, trans=1, unit_diagonal=True).reshape(length, head_count, length)
    moved_queries = queries_wide - jnp.einsum('thi,te->ihe', coefficients, scaled_dirs, precision=exact_mode)
    plain_scores = jnp.einsum('ihe,je->ihj', queries_wide, keys_wide, precision=exact_mode)
    correction = jnp.einsum('thi,tj->ihj', coefficients, beta[:, None] * key_reach, precision=exact_mode)
    local_scores = jnp.where(causal_mask[:, None, :], (plain_scores - correction) * head_width ** (-0.5), -1e+30)
    return (moved_queries, moved_keys, transform, local_scores)

def group_output(queries, keys, values, directions, beta, gain):
    grouped = queries.reshape(N_SEQ, TOK_DEV, GROUP_HEADS, HD)

    def local_terms(pieces):
        return segment_terms(pieces[0], pieces[1], pieces[2], pieces[3])
    moved_queries, moved_keys, transforms, local_scores = lax.map(local_terms, (grouped, keys.reshape(N_SEQ, TOK_DEV, HD), directions.reshape(N_SEQ, TOK_DEV, HD), beta.reshape(N_SEQ, TOK_DEV)))
    query_rows = moved_queries.reshape(N_SEQ, TOK_DEV * GROUP_HEADS, HD).astype(jnp.bfloat16)
    local_flat = local_scores.reshape(N_SEQ, TOK_DEV * GROUP_HEADS, TOK_DEV)
    key_travel = moved_keys.astype(jnp.bfloat16)
    hop_matrices = transforms.astype(jnp.bfloat16)
    value_blocks = values.reshape(N_SEQ, TOK_DEV, HD)
    positions = jnp.arange(TOKENS)

    def attend_segment(history, inputs):
        segment_index, query_block, local_block, own_keys, own_values, hop_matrix = inputs
        cross = jnp.dot(query_block.astype(jnp.float32), history.T.astype(jnp.float32), preferred_element_type=jnp.float32) * HD ** (-0.5)
        cross = jnp.where((positions < segment_index * TOK_DEV)[None, :], cross, -1e+30)
        scores = jnp.concatenate([cross, local_block], axis=1)
        peak = lax.optimization_barrier(jnp.max(scores, axis=1, keepdims=True))
        weights_exp = jnp.exp(scores - peak)
        denominator = lax.optimization_barrier(jnp.sum(weights_exp, axis=1, keepdims=True))
        mixed = jnp.dot(weights_exp.astype(jnp.bfloat16).astype(jnp.float32), jnp.concatenate([values, own_values], axis=0).astype(jnp.float32), preferred_element_type=jnp.float32) / denominator
        strength = lax.rsqrt(lax.optimization_barrier(jnp.mean(mixed * mixed, axis=1, keepdims=True)) + 1e-06)
        normed = (mixed * strength * gain[None, :]).astype(jnp.bfloat16)
        history = jnp.dot(history.astype(jnp.float32), hop_matrix.T.astype(jnp.float32), preferred_element_type=jnp.float32).astype(jnp.bfloat16)
        history = lax.dynamic_update_slice(history, own_keys, ((segment_index * TOK_DEV).astype(jnp.int32), jnp.int32(0)))
        return (history, normed)
    history = jnp.zeros((TOKENS, HD), jnp.bfloat16)
    indices = jnp.arange(N_SEQ, dtype=jnp.int32)
    final_history, outputs = lax.scan(attend_segment, history, (indices, query_rows, local_flat, key_travel, value_blocks, hop_matrices))
    return outputs.reshape(TOKENS, GROUP_HEADS * HD)

def reference(queries, keys, values, directions, beta, gain):
    query_groups = queries.reshape(TOKENS, GROUPS, GROUP_HEADS * HD).transpose(1, 0, 2)
    key_groups = keys.reshape(TOKENS, GROUPS, HD).transpose(1, 0, 2)
    value_groups = values.reshape(TOKENS, GROUPS, HD).transpose(1, 0, 2)
    direction_groups = directions.reshape(TOKENS, GROUPS, HD).transpose(1, 0, 2)
    beta_groups = beta.T

    def one_group(pieces):
        return group_output(pieces[0], pieces[1], pieces[2], pieces[3], pieces[4], gain)
    outputs = lax.map(one_group, (query_groups, key_groups, value_groups, direction_groups, beta_groups))
    return outputs.transpose(1, 0, 2).reshape(TOKENS, HEADS * HD)
```

```python
import functools
import math

import jax
import jax.numpy as jnp
from jax import lax
from jax.experimental import pallas as pl
from jax.experimental.pallas import tpu as pltpu
from jax.sharding import PartitionSpec as P

MESH = pl.DeviceIdType.MESH
F32 = jnp.float32
BF16 = jnp.bfloat16
NN = (((1,), (0,)), ((), ()))
NT = (((1,), (1,)), ((), ()))
LOW = -1e30
KW, VAL = 0, 1


def mm(a, b, dims=NN):
    return lax.dot_general(a, b, dims, preferred_element_type=F32)


def split(x):
    high = x.astype(BF16)
    return high, (x - high.astype(F32)).astype(BF16)


def mm3(a, b, dims=NN):
    return mm(a[0], b[0], dims) + (mm(a[0], b[1], dims) + mm(a[1], b[0], dims))


def kernel(
    chips, q_ref, k_ref, v_ref, u_ref, beta_ref, gain_ref, o_ref,
    got_u, got_k, got_v, own_seg, sib_seg, kw, val, q_rows, peak, total, acc, chain, keys_now,
    pair_send, pair_recv, line_send, line_recv, near_send, near_recv, ready,
):
    tokens, width = k_ref.shape[0], 2 * k_ref.shape[1]
    heads = q_ref.shape[1] // width
    half = width // 2
    factor = math.log2(math.e) / math.sqrt(width)
    s, h = lax.axis_index("seq"), lax.axis_index("head")
    z, c = lax.div(s, 2), lax.rem(s, 2)
    last = chips - 1

    def chip(place):
        return (place * 2 + c, h)

    partner = (s, h + 1 - 2 * lax.rem(h, 2))
    sibling = (s + 1 - 2 * c, h)

    barrier = pltpu.get_barrier_semaphore()

    def tell(sem, device):
        pl.semaphore_signal(sem, inc=1, device_id=device, device_id_type=MESH)

    tell(barrier, partner)
    tell(barrier, sibling)
    pl.when(z + 1 <= last)(lambda: tell(barrier, chip(z + 1)))
    pl.when(z + 2 <= last)(lambda: tell(barrier, chip(z + 2)))
    pl.when(z <= 1)(lambda: tell(barrier, chip(last)))
    pl.when(z == 0)(lambda: tell(barrier, chip(last - 1)))
    extra = jnp.where(z == last, 2, jnp.where(z == last - 1, 1, 0))
    pl.semaphore_wait(barrier, 2 + jnp.minimum(z, 2) + extra)
    pl.when(z >= 1)(lambda: tell(ready.at[0], chip(z - 1)))
    pl.when(z >= 2)(lambda: tell(ready.at[1], chip(z - 2)))
    pl.when(z == last)(lambda: tell(ready.at[2], chip(0)))
    pl.when(z == last)(lambda: tell(ready.at[3], chip(1)))
    pl.when(z == last - 1)(lambda: tell(ready.at[3], chip(0)))

    swaps = [
        pltpu.make_async_remote_copy(
            src, dst, pair_send.at[i], pair_recv.at[i], device_id=partner, device_id_type=MESH
        )
        for i, (src, dst) in enumerate(((u_ref, got_u), (k_ref, got_k), (v_ref, got_v)))
    ]
    for copy in swaps:
        copy.start()
    even = lax.rem(h, 2) == 0

    def joined(own, other):
        own, other = own[...].astype(F32), other[...].astype(F32)
        return jnp.where(
            even, jnp.concatenate([own, other], axis=1), jnp.concatenate([other, own], axis=1)
        )

    rows_i = lax.broadcasted_iota(jnp.int32, (tokens, tokens), 0)
    cols_i = lax.broadcasted_iota(jnp.int32, (tokens, tokens), 1)
    eye = (rows_i == cols_i).astype(F32)
    lane = lax.broadcasted_iota(jnp.int32, beta_ref.shape, 1)
    beta = jnp.sum(jnp.where(lane == lax.div(h, 2), beta_ref[...], 0.0), axis=1, keepdims=True)

    buffers = (kw, val)

    def line_copy(kind, source_slot, target_slot, device):
        return pltpu.make_async_remote_copy(
            buffers[kind].at[source_slot, c],
            buffers[kind].at[target_slot, c],
            line_send.at[kind, target_slot],
            line_recv.at[kind, target_slot],
            device_id=device,
            device_id_type=MESH,
        )

    def near_copy(kind, slot):
        return pltpu.make_async_remote_copy(
            buffers[kind].at[slot, c],
            buffers[kind].at[slot, c],
            near_send.at[kind, slot],
            near_recv.at[kind, slot],
            device_id=sibling,
            device_id_type=MESH,
        )

    def near_arrival(kind, slot):
        return pltpu.make_async_remote_copy(
            buffers[kind].at[slot, 1 - c],
            buffers[kind].at[slot, 1 - c],
            near_send.at[kind, slot],
            near_recv.at[kind, slot],
            device_id=sibling,
            device_id_type=MESH,
        )

    reach = chips // 2
    far = chips - reach - 1

    def forward_relays(kind, d, act):
        @pl.when((z >= d) & (d + 1 <= reach) & (z + 1 <= last))
        def _():
            act(line_copy(kind, d, d + 1, chip(z + 1)))

        @pl.when((z >= d) & (d + 2 <= reach) & (z + 2 <= last))
        def _():
            act(line_copy(kind, d, d + 2, chip(z + 2)))

    def backward_relays(kind, e, act):
        slot = lax.rem(chips - e, chips) if not isinstance(e, int) else (chips - e) % chips
        wrapped = z + e >= chips
        held = (z + e < far) | wrapped

        @pl.when(held & (wrapped | (z == 0)) & (e + 1 <= far))
        def _():
            act(line_copy(kind, slot, chips - e - 1, chip(lax.rem(z + chips - 1, chips))))

        @pl.when(held & (e + 2 < far))
        def _():
            act(line_copy(kind, slot, chips - e - 2, chip(lax.rem(z + chips - 2, chips))))

    def begin(copy):
        copy.start()

    def arrive(kind, slot):
        line_copy(kind, slot, slot, sibling).wait_recv()

    def receive(kind, m):
        d1, d2 = 2 * m + 1, 2 * m + 2

        @pl.when(z >= d2)
        def _():
            arrive(kind, d2)

        forward_relays(kind, d2, begin)
        pl.when(z >= d2)(lambda: near_copy(kind, d2).start())

        @pl.when((d2 < far) & ((z + d2 < far) | (z + d2 >= chips)))
        def _():
            arrive(kind, chips - d2)

        @pl.when(d2 < far)
        def _():
            backward_relays(kind, d2, begin)

        @pl.when(z >= d1)
        def _():
            arrive(kind, d1)
            near_copy(kind, d1).start()

        @pl.when((d2 < far) & (z + d2 >= chips))
        def _():
            near_copy(kind, chips - d2).start()

        @pl.when((d1 <= far) & (z + d1 >= chips))
        def _():
            arrive(kind, chips - d1)
            near_copy(kind, chips - d1).start()

    swaps[0].wait_recv()
    raw = joined(u_ref, got_u)
    unit = raw * lax.rsqrt(jnp.sum(raw * raw, axis=1, keepdims=True) + 1e-06)
    scaled = beta * unit
    unit2, scaled2 = split(unit), split(scaled)
    nil = jnp.where(rows_i > cols_i, mm3(scaled2, unit2, NT), 0.0)
    swaps[1].wait_recv()
    keys_wide = joined(k_ref, got_k)
    keys_own = keys_wide.astype(BF16)
    reach_t = jnp.where(
        cols_i > rows_i, mm(keys_own, scaled2[0], NT) + mm(keys_own, scaled2[1], NT), 0.0
    )
    swaps[2].wait_recv()
    val[0, pl.ds(c, 1)] = joined(v_ref, got_v).astype(BF16)[None]
    near_copy(VAL, 0).start()

    @pl.when(lax.rem(z, 2) == 1)
    def _():
        kw[pl.ds(z + 1, 1)] = jnp.zeros((1,) + kw.shape[1:], BF16)
        val[pl.ds(z + 1, 1)] = jnp.zeros((1,) + val.shape[1:], BF16)

    pl.when(z + 1 <= last)(lambda: pl.semaphore_wait(ready.at[0], 1))
    pl.when(z + 2 <= last)(lambda: pl.semaphore_wait(ready.at[1], 1))
    forward_relays(VAL, 0, begin)

    inverse = eye
    size = 1
    while size < tokens:
        bits = size.bit_length() - 1
        block_r, block_c = rows_i >> bits, cols_i >> bits
        corner = jnp.where(((block_r & 1) == 1) & (block_c == block_r - 1), nil, 0.0)
        if size == 1:
            inverse = eye - corner
        else:
            inv2 = split(inverse)
            inverse = inverse - mm3(split(mm3(inv2, split(corner))), inv2)
        size *= 2
    solved2 = split(
        mm3(split(jnp.concatenate([jnp.transpose(scaled), reach_t], axis=0)), split(inverse), NT)
    )
    ends = jnp.concatenate([eye, keys_wide], axis=0) - mm3(solved2, unit2)
    own_seg[...] = ends.astype(BF16)

    seg_swap = pltpu.make_async_remote_copy(
        own_seg, sib_seg, pair_send.at[3], pair_recv.at[3], device_id=sibling, device_id_type=MESH
    )
    seg_swap.start()
    seg_swap.wait_recv()
    first = c == 0
    own_hop, own_keys = own_seg[0:width, :], own_seg[width : width + tokens, :]
    sib_hop, sib_keys = sib_seg[0:width, :], sib_seg[width : width + tokens, :]
    moved = jnp.where(first, mm(own_keys, sib_hop), own_keys.astype(F32))
    hops = jnp.where(first, mm(own_hop, sib_hop), mm(sib_hop, own_hop))
    hops = jnp.where(first, hops[0:half, :], hops[half:, :])
    kw[0, pl.ds(c, 1)] = jnp.concatenate([moved, hops], axis=0).astype(BF16)[None]
    forward_relays(KW, 0, begin)

    pl.when(z <= 1)(lambda: pl.semaphore_wait(ready.at[3], 1))
    pl.when(z == 0)(lambda: pl.semaphore_wait(ready.at[2], 1))
    backward_relays(VAL, 0, begin)
    backward_relays(KW, 0, begin)

    values_own = val[0, pl.ds(c, 1)].reshape(tokens, width)
    sides = jnp.concatenate([unit2[0], unit2[1], keys_own], axis=0)
    for head in range(heads):
        span = slice(head * tokens, (head + 1) * tokens)
        q = q_ref[:, head * width : (head + 1) * width]
        products = mm(q, sides, NT)
        onto = products[:, 0:tokens] + products[:, tokens : 2 * tokens]
        onto2 = split(jnp.where(rows_i >= cols_i, onto, 0.0))
        taken = mm3(onto2, solved2, NT)
        q_rows[span, :] = (q.astype(F32) - taken[:, 0:width]).astype(BF16)
        scores = (products[:, 2 * tokens :] - taken[:, width:]) * factor
        scores = jnp.where(rows_i >= cols_i, scores, LOW)
        top = jnp.max(scores, axis=1, keepdims=True)
        weights = jnp.exp2(scores - top)
        peak[span, :] = jnp.broadcast_to(top, (tokens, width))
        total[span, :] = weights
        acc[span, :] = mm(weights.astype(BF16), values_own)

    def absorb(key_block, value_block, mask):
        for head in range(heads):
            span = slice(head * tokens, (head + 1) * tokens)
            scores = mask(mm(q_rows[span, :], key_block(), NT))
            old = peak[span, :]
            top = jnp.maximum(old, jnp.max(scores, axis=1, keepdims=True))
            fade = jnp.exp2(old - top)
            peak[span, :] = top
            parts = []
            sums = total[span, :] * fade
            for i in range(scores.shape[1] // width):
                weights = jnp.exp2(scores[:, i * width : (i + 1) * width] - top)
                sums = sums + weights
                parts.append(weights.astype(BF16))
            total[span, :] = sums
            both = jnp.concatenate(parts, axis=1) if len(parts) > 1 else parts[0]
            acc[span, :] = acc[span, :] * fade + mm(both, value_block())

    near_arrival(VAL, 0).wait_recv()

    @pl.when(c == 1)
    def _():
        keys_now[0:tokens, :] = (sib_seg[width : width + tokens, :].astype(F32) * factor).astype(BF16)
        absorb(lambda: keys_now[0:tokens, :], lambda: val[0, 0], lambda x: x)

    chain[...] = jnp.where(first, eye, sib_seg[0:width, :].astype(F32)).astype(BF16)
    receive(VAL, 0)

    @pl.loop(0, (chips + 1) // 2)
    def _(m):
        @pl.when(2 * m < reach)
        def _():
            receive(KW, m)

        @pl.when(2 * m + 2 < reach)
        def _():
            receive(VAL, m + 1)

        @pl.when(z >= 2 * m + 1)
        def _():
            d1, d2 = 2 * m + 1, 2 * m + 2
            for kind in (KW, VAL):
                near_arrival(kind, d1).wait_recv()
                pl.when(z >= d2)(lambda kind=kind: near_arrival(kind, d2).wait_recv())
            for i, d in enumerate((d1, d2)):
                now = chain[...]
                for core in range(2):
                    block = mm(kw[d, core, 0:tokens, :], now) * factor
                    at = (2 * i + core) * tokens
                    keys_now[at : at + tokens, :] = block.astype(BF16)
                hop = jnp.concatenate(
                    [kw[d, 0, tokens : tokens + half, :], kw[d, 1, tokens : tokens + half, :]], axis=0
                )
                chain[...] = mm(hop, now).astype(BF16)
            both = z >= d2

            def mask(scores):
                n = 2 * tokens
                return jnp.concatenate(
                    [scores[:, 0:n], jnp.where(both, scores[:, n:], LOW)], axis=1
                )

            absorb(
                lambda: keys_now[...],
                lambda: val[pl.ds(d1, 2)].reshape(4 * tokens, width),
                mask,
            )

    gain = gain_ref[...]
    for head in range(heads):
        span = slice(head * tokens, (head + 1) * tokens)
        mixed = acc[span, :] / jnp.sum(total[span, :], axis=1, keepdims=True)
        strength = lax.rsqrt(jnp.mean(mixed * mixed, axis=1, keepdims=True) + 1e-06)
        o_ref[:, head * width : (head + 1) * width] = (mixed * strength * gain).astype(BF16)

    def left(copy):
        copy.wait_send()

    for copy in swaps:
        copy.wait_send()
    seg_swap.wait_send()
    near_copy(VAL, 0).wait_send()

    @pl.loop(0, reach // 2)
    def _(m):
        for kind in (KW, VAL):
            forward_relays(kind, 2 * m, left)

            @pl.when(2 * m < far)
            def _(kind=kind):
                backward_relays(kind, 2 * m, left)

    @pl.loop(1, chips)
    def _(d):
        for kind in (KW, VAL):
            pl.when(z >= d)(lambda kind=kind: near_copy(kind, d).wait_send())


def solution(mesh):
    chips = mesh.shape["seq"] // 2

    def step(q, k, v, u, beta, gain):
        tokens, width = k.shape[0], 2 * k.shape[1]
        rows = tokens * (q.shape[1] // width)
        slots = chips + 1
        vmem = pl.BlockSpec(memory_space=pltpu.VMEM)
        piece = tokens + width // 2
        return pl.pallas_call(
            functools.partial(kernel, chips),
            out_shape=jax.ShapeDtypeStruct(q.shape, BF16),
            in_specs=[vmem] * 6,
            out_specs=vmem,
            scratch_shapes=[
                pltpu.VMEM(k.shape, BF16),
                pltpu.VMEM(k.shape, BF16),
                pltpu.VMEM(k.shape, BF16),
                pltpu.VMEM((width + tokens, width), BF16),
                pltpu.VMEM((width + tokens, width), BF16),
                pltpu.VMEM((slots, 2, piece, width), BF16),
                pltpu.VMEM((slots, 2, tokens, width), BF16),
                pltpu.VMEM((rows, width), BF16),
                pltpu.VMEM((rows, width), F32),
                pltpu.VMEM((rows, width), F32),
                pltpu.VMEM((rows, width), F32),
                pltpu.VMEM((width, width), BF16),
                pltpu.VMEM((4 * tokens, width), BF16),
                pltpu.SemaphoreType.DMA((4,)),
                pltpu.SemaphoreType.DMA((4,)),
                pltpu.SemaphoreType.DMA((2, slots)),
                pltpu.SemaphoreType.DMA((2, slots)),
                pltpu.SemaphoreType.DMA((2, slots)),
                pltpu.SemaphoreType.DMA((2, slots)),
                pltpu.SemaphoreType.REGULAR((4,)),
            ],
            compiler_params=pltpu.CompilerParams(
                collective_id=0, has_side_effects=True, vmem_limit_bytes=40 * 2**20
            ),
        )(q, k, v, u, beta, gain.reshape(1, width))

    return jax.shard_map(
        step,
        mesh=mesh,
        in_specs=(P("seq", "head"),) * 4 + (P("seq", None), P()),
        out_specs=P("seq", "head"),
        check_vma=False,
    )
```

```python
import functools
import math

import jax
import jax.numpy as jnp
from jax import lax
from jax.experimental import pallas as pl
from jax.experimental.pallas import tpu as pltpu
from jax.sharding import PartitionSpec as P

MESH = pl.DeviceIdType.MESH
F32 = jnp.float32
BF16 = jnp.bfloat16
NN = (((1,), (0,)), ((), ()))
NT = (((1,), (1,)), ((), ()))
LOW = -1e30
KW, VAL = 0, 1


def mm(a, b, dims=NN):
    return lax.dot_general(a, b, dims, preferred_element_type=F32)


def split(x):
    high = x.astype(BF16)
    return high, (x - high.astype(F32)).astype(BF16)


def mm3(a, b, dims=NN):
    return mm(a[0], b[0], dims) + (mm(a[0], b[1], dims) + mm(a[1], b[0], dims))


def kernel(
    chips, q_ref, k_ref, v_ref, u_ref, beta_ref, gain_ref, o_ref,
    q_own, whole, beta_own, gain_own, own_seg, sib_seg, kw, val, q_rows, peak, total, acc, chain, keys_now, far_keys,
    local, pair_send, pair_recv, line_send, line_recv, near_send, near_recv, cross_send, cross_recv, ready,
):
    half, tokens = k_ref.shape
    width = 2 * half
    heads = q_ref.shape[1] // width
    factor = math.log2(math.e) / math.sqrt(width)
    s, h = lax.axis_index("seq"), lax.axis_index("head")
    z, c = lax.div(s, 2), lax.rem(s, 2)
    last = chips - 1

    def chip(place):
        return (place * 2 + c, h)

    partner = (s, h + 1 - 2 * lax.rem(h, 2))
    sibling = (s + 1 - 2 * c, h)

    parity = lax.rem(h, 2)
    own_rows = pl.ds(parity * half, half)
    halves = (u_ref, k_ref, v_ref)
    loads = [
        pltpu.make_async_copy(src, dst, local.at[i])
        for i, (src, dst) in enumerate(
            [(src, whole.at[i, own_rows]) for i, src in enumerate(halves)]
            + [(beta_ref, beta_own), (gain_ref, gain_own), (q_ref, q_own)]
        )
    ]
    for copy in loads:
        copy.start()

    barrier = pltpu.get_barrier_semaphore()

    def tell(sem, device):
        pl.semaphore_signal(sem, inc=1, device_id=device, device_id_type=MESH)

    tell(barrier, partner)
    tell(barrier, sibling)
    pl.when(z + 1 <= last)(lambda: tell(barrier, chip(z + 1)))
    pl.when(z + 2 <= last)(lambda: tell(barrier, chip(z + 2)))
    pl.when(z <= 1)(lambda: tell(barrier, chip(last)))
    pl.when(z == 0)(lambda: tell(barrier, chip(last - 1)))
    extra = jnp.where(z == last, 2, jnp.where(z == last - 1, 1, 0))
    pl.semaphore_wait(barrier, 2 + jnp.minimum(z, 2) + extra)
    pl.when(z >= 1)(lambda: tell(ready.at[0], chip(z - 1)))
    pl.when(z >= 2)(lambda: tell(ready.at[1], chip(z - 2)))
    pl.when(z == last)(lambda: tell(ready.at[2], chip(0)))
    pl.when(z == last)(lambda: tell(ready.at[3], chip(1)))
    pl.when(z == last - 1)(lambda: tell(ready.at[3], chip(0)))

    swaps = [
        pltpu.make_async_remote_copy(
            src, whole.at[i, own_rows], pair_send.at[i], pair_recv.at[i],
            device_id=partner, device_id_type=MESH,
        )
        for i, src in enumerate(halves)
    ]
    for copy in swaps:
        copy.start()

    rows_i = lax.broadcasted_iota(jnp.int32, (tokens, tokens), 0)
    cols_i = lax.broadcasted_iota(jnp.int32, (tokens, tokens), 1)
    eye = (rows_i == cols_i).astype(F32)

    def swapped(i):
        rows = pl.ds((1 - parity) * half, half)
        loads[i].wait()
        pltpu.make_async_remote_copy(
            halves[i], whole.at[i, rows], pair_send.at[i], pair_recv.at[i],
            device_id=partner, device_id_type=MESH,
        ).wait_recv()
        return whole[i]

    buffers = (kw, val)

    def line_copy(kind, source_slot, target_slot, device):
        return pltpu.make_async_remote_copy(
            buffers[kind].at[source_slot, c],
            buffers[kind].at[target_slot, c],
            line_send.at[kind, target_slot],
            line_recv.at[kind, target_slot],
            device_id=device,
            device_id_type=MESH,
        )

    def near_copy(kind, slot):
        return pltpu.make_async_remote_copy(
            buffers[kind].at[slot, c],
            buffers[kind].at[slot, c],
            near_send.at[kind, slot],
            near_recv.at[kind, slot],
            device_id=sibling,
            device_id_type=MESH,
        )

    def near_arrival(kind, slot):
        return pltpu.make_async_remote_copy(
            buffers[kind].at[slot, 1 - c],
            buffers[kind].at[slot, 1 - c],
            near_send.at[kind, slot],
            near_recv.at[kind, slot],
            device_id=sibling,
            device_id_type=MESH,
        )

    def cross_copy(kind, slot):
        return pltpu.make_async_remote_copy(
            buffers[kind].at[slot, c],
            buffers[kind].at[slot, c],
            cross_send.at[kind, slot],
            cross_recv.at[kind, slot],
            device_id=partner,
            device_id_type=MESH,
        )

    reach = chips // 2
    far = chips - reach - 1
    farthest = far - 1 + parity

    def push_forward(kind, m, act):
        goal = 2 * m + 2 - parity
        if isinstance(m, int) and m == 0:
            fits, source, place = z + goal <= last, 0, z + goal
        else:
            fits = (z >= goal - 2) & (z + 2 <= last) & (goal <= reach)
            source, place = goal - 2, z + 2

        @pl.when(fits)
        def _():
            act(line_copy(kind, source, goal, chip(place)))

    def passing(e):
        return (z + e >= chips) | (z + e < farthest)

    def push_backward(kind, m, act):
        goal = 2 * m + 2 - parity
        if isinstance(m, int) and m == 0:
            fits, source, place = z < farthest, 0, z + chips - goal
        else:
            fits = passing(goal - 2) & (goal <= farthest)
            source, place = chips + 2 - goal, z + chips - 2

        @pl.when(fits)
        def _():
            act(line_copy(kind, source, chips - goal, chip(lax.rem(place, chips))))

    def begin(copy):
        copy.start()

    def arrive(kind, slot):
        line_copy(kind, slot, slot, sibling).wait_recv()

    def spread(kind, slot):
        cross_copy(kind, slot).start()
        near_copy(kind, slot).start()

    def line_stage(kind, m):
        d = 2 * m + 2 - parity
        pl.when(z >= d)(lambda: arrive(kind, d))
        push_forward(kind, m + 1, begin)
        pl.when(z >= d)(lambda: spread(kind, d))
        inside = d <= farthest
        pl.when(inside & passing(d))(lambda: arrive(kind, chips - d))
        push_backward(kind, m + 1, begin)
        pl.when(inside & (z + d >= chips))(lambda: spread(kind, chips - d))

    def cross_stage(kind, m):
        d = 2 * m + 1 + parity

        def take(slot):
            cross_copy(kind, slot).wait_recv()
            near_copy(kind, slot).start()

        pl.when(z >= d)(lambda: take(d))
        pl.when((d <= far - parity) & (z + d >= chips))(lambda: take(chips - d))

    def clear(slot):
        kw[pl.ds(slot, 1)] = jnp.zeros((1,) + kw.shape[1:], BF16)
        val[pl.ds(slot, 1)] = jnp.zeros((1,) + val.shape[1:], BF16)

    pl.when((lax.rem(z, 2) == 1) & (z < reach))(lambda: clear(z + 1))

    @pl.when(z > reach)
    def _():
        @pl.loop(z + 1, chips)
        def _(slot):
            clear(slot)

    loads[3].wait()
    lane = lax.broadcasted_iota(jnp.int32, beta_ref.shape, 0)
    beta = jnp.sum(jnp.where(lane == lax.div(h, 2), beta_own[...], 0.0), axis=0, keepdims=True)
    raw_t = swapped(0).astype(F32)
    unit_t = raw_t * lax.rsqrt(jnp.sum(raw_t * raw_t, axis=0, keepdims=True) + 1e-06)
    scaled_t = beta * unit_t
    unit2, scaled_t2 = split(jnp.transpose(unit_t)), split(scaled_t)
    upper = cols_i > rows_i
    nil_t = jnp.where(upper, mm3(unit2, scaled_t2), 0.0)
    keys_t = swapped(1)
    keys_wide = jnp.transpose(keys_t.astype(F32))
    keys_own = keys_wide.astype(BF16)
    reach_t = jnp.where(upper, mm(keys_own, scaled_t2[0]) + mm(keys_own, scaled_t2[1]), 0.0)
    val[0, pl.ds(c, 1)] = jnp.transpose(swapped(2).astype(F32)).astype(BF16)[None]
    near_copy(VAL, 0).start()

    pl.when(z + 1 <= last)(lambda: pl.semaphore_wait(ready.at[0], 1))
    pl.when(z + 2 <= last)(lambda: pl.semaphore_wait(ready.at[1], 1))
    push_forward(VAL, 0, begin)

    inverse = eye
    size = 1
    while size < tokens:
        bits = size.bit_length() - 1
        block_r, block_c = rows_i >> bits, cols_i >> bits
        corner = jnp.where(((block_c & 1) == 1) & (block_r == block_c - 1), nil_t, 0.0)
        if size == 1:
            inverse = eye - corner
        else:
            inv2 = split(inverse)
            inverse = inverse - mm3(split(mm3(inv2, split(corner))), inv2)
        size *= 2
    solved2 = split(mm3(split(jnp.concatenate([scaled_t, reach_t], axis=0)), split(inverse)))
    ends = jnp.concatenate([eye, keys_wide], axis=0) - mm3(solved2, unit2)
    own_seg[...] = ends.astype(BF16)

    seg_swap = pltpu.make_async_remote_copy(
        own_seg, sib_seg, pair_send.at[3], pair_recv.at[3], device_id=sibling, device_id_type=MESH
    )
    seg_swap.start()
    seg_swap.wait_recv()
    first = c == 0
    own_hop, own_keys = own_seg[0:width, :], own_seg[width : width + tokens, :]
    sib_hop, sib_keys = sib_seg[0:width, :], sib_seg[width : width + tokens, :]
    moved = jnp.where(first, mm(own_keys, sib_hop), own_keys.astype(F32))
    hops = jnp.where(first, mm(own_hop, sib_hop), mm(sib_hop, own_hop))
    hops = jnp.where(first, hops[0:half, :], hops[half:, :])
    kw[0, pl.ds(c, 1)] = jnp.concatenate([moved, hops], axis=0).astype(BF16)[None]
    push_forward(KW, 0, begin)

    pl.when(z <= 1)(lambda: pl.semaphore_wait(ready.at[3], 1))
    pl.when(z == 0)(lambda: pl.semaphore_wait(ready.at[2], 1))
    push_backward(VAL, 0, begin)
    push_backward(KW, 0, begin)

    line_stage(VAL, 0)

    loads[5].wait()
    for head in range(heads):
        q_rows[head * tokens : (head + 1) * tokens, :] = q_own[:, head * width : (head + 1) * width]
    values_own = val[0, pl.ds(c, 1)].reshape(tokens, width)
    unit_t2 = split(unit_t)
    q = q_rows[...]
    products = mm(q, jnp.concatenate([unit_t2[0], unit_t2[1], keys_t], axis=1))
    causal = jnp.concatenate([rows_i >= cols_i] * heads, axis=0)
    onto = products[:, 0:tokens] + products[:, tokens : 2 * tokens]
    taken = mm3(split(jnp.where(causal, onto, 0.0)), solved2, NT)
    q_rows[...] = (q.astype(F32) - taken[:, 0:width]).astype(BF16)
    scores = (products[:, 2 * tokens :] - taken[:, width:]) * factor
    scores = jnp.where(causal, scores, LOW)
    top = jnp.max(scores, axis=1, keepdims=True)
    weights = jnp.exp2(scores - top)
    peak[...] = jnp.broadcast_to(top, peak.shape)
    total[...] = weights
    acc[...] = mm(weights.astype(BF16), values_own)

    def absorb(key_block, value_block, mask):
        scores = mask(mm(q_rows[...], key_block(), NT))
        old = peak[...]
        top = jnp.maximum(old, jnp.max(scores, axis=1, keepdims=True))
        fade = jnp.exp2(old - top)
        peak[...] = top
        parts = []
        sums = total[...] * fade
        for i in range(scores.shape[1] // width):
            weights = jnp.exp2(scores[:, i * width : (i + 1) * width] - top)
            sums = sums + weights
            parts.append(weights.astype(BF16))
        total[...] = sums
        both = jnp.concatenate(parts, axis=1) if len(parts) > 1 else parts[0]
        acc[...] = acc[...] * fade + mm(both, value_block())

    near_arrival(VAL, 0).wait_recv()

    @pl.when(c == 1)
    def _():
        keys_now[0:tokens, :] = (sib_seg[width : width + tokens, :].astype(F32) * factor).astype(BF16)
        absorb(lambda: keys_now[0:tokens, :], lambda: val[0, 0], lambda x: x)

    chain[...] = jnp.where(first, eye, sib_seg[0:width, :].astype(F32)).astype(BF16)

    def hop_of(d):
        return jnp.concatenate(
            [kw[d, 0, tokens : tokens + half, :], kw[d, 1, tokens : tokens + half, :]], axis=0
        )

    def await_block(d):
        for kind in (KW, VAL):
            near_arrival(kind, d).wait_recv()

    @pl.loop(0, reach // 2 + 1)
    def _(i):
        m = i - 1

        @pl.when(2 * i < reach)
        def _():
            line_stage(KW, i)

        @pl.when(2 * i + 2 < reach)
        def _():
            line_stage(VAL, i + 1)

        @pl.when(i >= 1)
        def _():
            cross_stage(KW, m)
            cross_stage(VAL, m)

        @pl.when((i >= 1) & (z >= 2 * m + 1))
        def _():
            d1, d2 = 2 * m + 1, 2 * m + 2
            await_block(d1)
            pl.when(z >= d2)(lambda: await_block(d2))
            for j, d in enumerate((d1, d2)):
                now = chain[...]
                for core in range(2):
                    block = mm(kw[d, core, 0:tokens, :], now) * factor
                    at = (2 * j + core) * tokens
                    keys_now[at : at + tokens, :] = block.astype(BF16)
                chain[...] = mm(hop_of(d), now).astype(BF16)
            both = z >= d2

            def mask(scores):
                n = 2 * tokens
                return jnp.concatenate([scores[:, 0:n], jnp.where(both, scores[:, n:], LOW)], axis=1)

            absorb(
                lambda: keys_now[...],
                lambda: val[pl.ds(d1, 2)].reshape(4 * tokens, width),
                mask,
            )

    nearest, block = reach + 1, 2 * tokens

    @pl.when(z >= nearest)
    def _():
        for d in range(nearest, chips):
            pl.when(z >= d)(lambda d=d: await_block(d))
        so_far = None
        for d in range(nearest + 1, chips):
            at = (d - nearest) * block
            if so_far is None:
                for core in range(2):
                    far_keys[at + core * tokens : at + (core + 1) * tokens, :] = kw[d, core, 0:tokens, :]
                so_far = hop_of(d)
            else:
                for core in range(2):
                    far_keys[at + core * tokens : at + (core + 1) * tokens, :] = mm(
                        kw[d, core, 0:tokens, :], so_far
                    ).astype(BF16)
                so_far = mm(hop_of(d), so_far).astype(BF16)
        now = chain[...]
        for core in range(2):
            far_keys[core * tokens : (core + 1) * tokens, :] = (
                mm(kw[nearest, core, 0:tokens, :], now) * factor
            ).astype(BF16)
        beyond = mm(hop_of(nearest), now).astype(BF16)
        far_keys[block:, :] = (mm(far_keys[block:, :], beyond) * factor).astype(BF16)

        def mask(scores):
            return jnp.concatenate(
                [
                    jnp.where(z >= nearest + i, scores[:, i * block : (i + 1) * block], LOW)
                    for i in range(chips - nearest)
                ],
                axis=1,
            )

        absorb(
            lambda: far_keys[...],
            lambda: val[nearest:chips].reshape((chips - nearest) * block, width),
            mask,
        )

    loads[4].wait()
    gain = gain_own[...]
    for head in range(heads):
        span = slice(head * tokens, (head + 1) * tokens)
        mixed = acc[span, :] / jnp.sum(total[span, :], axis=1, keepdims=True)
        strength = lax.rsqrt(jnp.mean(mixed * mixed, axis=1, keepdims=True) + 1e-06)
        o_ref[:, head * width : (head + 1) * width] = (mixed * strength * gain).astype(BF16)

    def left(copy):
        copy.wait_send()

    for copy in swaps:
        copy.wait_send()
    seg_swap.wait_send()
    near_copy(VAL, 0).wait_send()

    for kind in (KW, VAL):
        push_forward(kind, 0, left)
        push_backward(kind, 0, left)

        @pl.loop(1, reach // 2)
        def _(m, kind=kind):
            push_forward(kind, m, left)
            push_backward(kind, m, left)

        @pl.loop(1, chips)
        def _(d, kind=kind):
            @pl.when(z >= d)
            def _():
                near_copy(kind, d).wait_send()
                pl.when(lax.rem(d, 2) == parity)(lambda: cross_copy(kind, d).wait_send())


def solution(mesh):
    chips = mesh.shape["seq"] // 2

    def step(q, k, v, u, beta, gain):
        tokens, width = k.shape[0], 2 * k.shape[1]
        rows = tokens * (q.shape[1] // width)
        slots = chips + 1
        piece = tokens + width // 2
        return pl.pallas_call(
            functools.partial(kernel, chips),
            out_shape=jax.ShapeDtypeStruct(q.shape, BF16),
            in_specs=[pl.BlockSpec(memory_space=pltpu.HBM)] * 6,
            out_specs=pl.BlockSpec(memory_space=pltpu.VMEM),
            scratch_shapes=[
                pltpu.VMEM(q.shape, BF16),
                pltpu.VMEM((3, width, tokens), BF16),
                pltpu.VMEM((beta.shape[1], tokens), F32),
                pltpu.VMEM((1, width), F32),
                pltpu.VMEM((width + tokens, width), BF16),
                pltpu.VMEM((width + tokens, width), BF16),
                pltpu.VMEM((slots, 2, piece, width), BF16),
                pltpu.VMEM((slots, 2, tokens, width), BF16),
                pltpu.VMEM((rows, width), BF16),
                pltpu.VMEM((rows, width), F32),
                pltpu.VMEM((rows, width), F32),
                pltpu.VMEM((rows, width), F32),
                pltpu.VMEM((width, width), BF16),
                pltpu.VMEM((4 * tokens, width), BF16),
                pltpu.VMEM(((chips - chips // 2 - 1) * 2 * tokens, width), BF16),
                pltpu.SemaphoreType.DMA((6,)),
                pltpu.SemaphoreType.DMA((4,)),
                pltpu.SemaphoreType.DMA((4,)),
                pltpu.SemaphoreType.DMA((2, slots)),
                pltpu.SemaphoreType.DMA((2, slots)),
                pltpu.SemaphoreType.DMA((2, slots)),
                pltpu.SemaphoreType.DMA((2, slots)),
                pltpu.SemaphoreType.DMA((2, slots)),
                pltpu.SemaphoreType.DMA((2, slots)),
                pltpu.SemaphoreType.REGULAR((4,)),
            ],
            compiler_params=pltpu.CompilerParams(
                collective_id=0, has_side_effects=True, vmem_limit_bytes=60 * 2**20
            ),
        )(q, k.T, v.T, u.T, beta.T, gain.reshape(1, width))

    return jax.shard_map(
        step,
        mesh=mesh,
        in_specs=(P("seq", "head"),) * 4 + (P("seq", None), P()),
        out_specs=P("seq", "head"),
        check_vma=False,
    )
```

```python
import functools
import math

import jax
import jax.numpy as jnp
from jax import lax
from jax.experimental import pallas as pl
from jax.experimental.pallas import tpu as pltpu
from jax.sharding import PartitionSpec as P

MESH = pl.DeviceIdType.MESH
F32 = jnp.float32
BF16 = jnp.bfloat16
NN = (((1,), (0,)), ((), ()))
NT = (((1,), (1,)), ((), ()))
LOW = -1e30
KEY, VAL = 0, 1


def mm(a, b, dims=NN):
    return lax.dot_general(a, b, dims, preferred_element_type=F32)


def split(x):
    high = x.astype(BF16)
    return high, (x - high.astype(F32)).astype(BF16)


def mm3(a, b, dims=NN):
    return mm(a[0], b[0], dims) + (mm(a[0], b[1], dims) + mm(a[1], b[0], dims))


def kernel(
    chips, q_ref, k_ref, v_ref, u_ref, beta_ref, gain_ref, o_ref,
    q_own, whole, beta_own, gain_own, own_seg, sib_seg, key, val, q_rows, peak, total, acc, chain, keys_now, far_keys,
    local, pair_send, pair_recv, line_send, line_recv, near_send, near_recv, cross_send, cross_recv, ready,
):
    half, tokens = k_ref.shape
    width = 2 * half
    heads = q_ref.shape[1] // width
    factor = math.log2(math.e) / math.sqrt(width)
    s, h = lax.axis_index("seq"), lax.axis_index("head")
    z, c = lax.div(s, 2), lax.rem(s, 2)
    last = chips - 1

    def chip(place):
        return (place * 2 + c, h)

    partner = (s, h + 1 - 2 * lax.rem(h, 2))
    sibling = (s + 1 - 2 * c, h)

    parity = lax.rem(h, 2)
    own_rows = pl.ds(parity * half, half)
    halves = (u_ref, k_ref, v_ref)
    loads = [
        pltpu.make_async_copy(src, dst, local.at[i])
        for i, (src, dst) in enumerate(
            [(src, whole.at[i, own_rows]) for i, src in enumerate(halves)]
            + [(beta_ref, beta_own), (gain_ref, gain_own), (q_ref, q_own)]
        )
    ]
    for copy in loads:
        copy.start()

    barrier = pltpu.get_barrier_semaphore()

    def tell(sem, device):
        pl.semaphore_signal(sem, inc=1, device_id=device, device_id_type=MESH)

    tell(barrier, partner)
    tell(barrier, sibling)
    pl.when(z + 1 <= last)(lambda: tell(barrier, chip(z + 1)))
    pl.when(z + 2 <= last)(lambda: tell(barrier, chip(z + 2)))
    pl.when(z <= 1)(lambda: tell(barrier, chip(last)))
    pl.when(z == 0)(lambda: tell(barrier, chip(last - 1)))
    extra = jnp.where(z == last, 2, jnp.where(z == last - 1, 1, 0))
    pl.semaphore_wait(barrier, 2 + jnp.minimum(z, 2) + extra)
    pl.when(z >= 1)(lambda: tell(ready.at[0], chip(z - 1)))
    pl.when(z >= 2)(lambda: tell(ready.at[1], chip(z - 2)))
    pl.when(z == last)(lambda: tell(ready.at[2], chip(0)))
    pl.when(z == last)(lambda: tell(ready.at[3], chip(1)))
    pl.when(z == last - 1)(lambda: tell(ready.at[3], chip(0)))

    swaps = [
        pltpu.make_async_remote_copy(
            src, whole.at[i, own_rows], pair_send.at[i], pair_recv.at[i],
            device_id=partner, device_id_type=MESH,
        )
        for i, src in enumerate(halves)
    ]
    for copy in swaps:
        copy.start()

    rows_i = lax.broadcasted_iota(jnp.int32, (tokens, tokens), 0)
    cols_i = lax.broadcasted_iota(jnp.int32, (tokens, tokens), 1)
    eye = (rows_i == cols_i).astype(F32)

    def swapped(i):
        rows = pl.ds((1 - parity) * half, half)
        loads[i].wait()
        pltpu.make_async_remote_copy(
            halves[i], whole.at[i, rows], pair_send.at[i], pair_recv.at[i],
            device_id=partner, device_id_type=MESH,
        ).wait_recv()
        return whole[i]

    buffers = (key, val)

    def line_copy(kind, source_slot, target_slot, device):
        return pltpu.make_async_remote_copy(
            buffers[kind].at[source_slot, c, parity],
            buffers[kind].at[target_slot, c, parity],
            line_send.at[kind, target_slot],
            line_recv.at[kind, target_slot],
            device_id=device,
            device_id_type=MESH,
        )

    part = tokens // 2

    def near_piece(kind, slot, core):
        return buffers[kind].at[slot, core]

    def near_transfer(kind, slot, core):
        return pltpu.make_async_remote_copy(
            near_piece(kind, slot, core),
            near_piece(kind, slot, core),
            near_send.at[kind, slot],
            near_recv.at[kind, slot],
            device_id=sibling,
            device_id_type=MESH,
        )

    def near_copy(kind, slot):
        return near_transfer(kind, slot, c)

    def near_arrival(kind, slot):
        return near_transfer(kind, slot, 1 - c)

    def cross_copy(kind, slot, side):
        return pltpu.make_async_remote_copy(
            buffers[kind].at[slot, c, side],
            buffers[kind].at[slot, c, side],
            cross_send.at[kind, slot],
            cross_recv.at[kind, slot],
            device_id=partner,
            device_id_type=MESH,
        )

    reach = chips // 2
    far = chips - reach - 1

    def forward_relays(kind, d, act):
        @pl.when((z >= d) & (d + 1 <= reach) & (z + 1 <= last))
        def _():
            act(line_copy(kind, d, d + 1, chip(z + 1)))

        @pl.when((z >= d) & (d + 2 <= reach) & (z + 2 <= last))
        def _():
            act(line_copy(kind, d, d + 2, chip(z + 2)))

    def backward_relays(kind, e, act):
        slot = lax.rem(chips - e, chips)
        wrapped = z + e >= chips
        held = (z + e < far) | wrapped

        @pl.when(held & (wrapped | (z == 0)) & (e + 1 <= far))
        def _():
            act(line_copy(kind, slot, chips - e - 1, chip(lax.rem(z + chips - 1, chips))))

        @pl.when(held & (e + 2 < far))
        def _():
            act(line_copy(kind, slot, chips - e - 2, chip(lax.rem(z + chips - 2, chips))))

    def begin(copy):
        copy.start()

    def arrive(kind, slot):
        line_copy(kind, slot, slot, sibling).wait_recv()

    def spread(kind, slot):
        cross_copy(kind, slot, parity).start()

    def line_stage(kind, m):
        d1, d2 = 2 * m + 1, 2 * m + 2
        pl.when(z >= d2)(lambda: arrive(kind, d2))
        forward_relays(kind, d2, begin)
        pl.when(z >= d2)(lambda: spread(kind, d2))

        @pl.when(z >= d1)
        def _():
            arrive(kind, d1)
            spread(kind, d1)

        @pl.when((d2 < far) & ((z + d2 < far) | (z + d2 >= chips)))
        def _():
            arrive(kind, chips - d2)

        @pl.when(d2 < far)
        def _():
            backward_relays(kind, d2, begin)

        @pl.when((d2 < far) & (z + d2 >= chips))
        def _():
            spread(kind, chips - d2)

        @pl.when((d1 <= far) & (z + d1 >= chips))
        def _():
            arrive(kind, chips - d1)
            spread(kind, chips - d1)

    def cross_stage(kind, m):
        d1, d2 = 2 * m + 1, 2 * m + 2

        def take(slot):
            cross_copy(kind, slot, 1 - parity).wait_recv()
            near_copy(kind, slot).start()

        pl.when(z >= d1)(lambda: take(d1))
        pl.when(z >= d2)(lambda: take(d2))
        pl.when((d2 < far) & (z + d2 >= chips))(lambda: take(chips - d2))
        pl.when((d1 <= far) & (z + d1 >= chips))(lambda: take(chips - d1))

    def clear(slot):
        for buffer in buffers:
            buffer[pl.ds(slot, 1)] = jnp.zeros((1,) + buffer.shape[1:], BF16)

    pl.when((lax.rem(z, 2) == 1) & (z < reach - 1))(lambda: clear(z + 1))

    @pl.when(z >= reach - 1)
    def _():
        @pl.loop(z + 1, chips)
        def _(slot):
            clear(slot)

    loads[3].wait()
    lane = lax.broadcasted_iota(jnp.int32, beta_ref.shape, 0)
    beta = jnp.sum(jnp.where(lane == lax.div(h, 2), beta_own[...], 0.0), axis=0, keepdims=True)
    raw_t = swapped(0).astype(F32)
    unit_t = raw_t * lax.rsqrt(jnp.sum(raw_t * raw_t, axis=0, keepdims=True) + 1e-06)
    scaled_t = beta * unit_t
    unit2, scaled_t2 = split(jnp.transpose(unit_t)), split(scaled_t)
    upper = cols_i > rows_i
    nil_t = jnp.where(upper, mm3(unit2, scaled_t2), 0.0)
    keys_t = swapped(1)
    keys_wide = jnp.transpose(keys_t.astype(F32))
    keys_own = keys_wide.astype(BF16)
    reach_t = jnp.where(upper, mm(keys_own, scaled_t2[0]) + mm(keys_own, scaled_t2[1]), 0.0)
    values_own = jnp.transpose(swapped(2).astype(F32)).astype(BF16)
    val[0, pl.ds(c, 1)] = values_own.reshape((1,) + val.shape[2:])
    near_copy(VAL, 0).start()

    pl.when(z + 1 <= last)(lambda: pl.semaphore_wait(ready.at[0], 1))
    pl.when(z + 2 <= last)(lambda: pl.semaphore_wait(ready.at[1], 1))
    forward_relays(VAL, 0, begin)

    inverse = eye
    size = 1
    while size < tokens:
        bits = size.bit_length() - 1
        block_r, block_c = rows_i >> bits, cols_i >> bits
        corner = jnp.where(((block_c & 1) == 1) & (block_r == block_c - 1), nil_t, 0.0)
        if size == 1:
            inverse = eye - corner
        else:
            inv2 = split(inverse)
            inverse = inverse - mm3(split(mm3(inv2, split(corner))), inv2)
        size *= 2
    solved2 = split(mm3(split(jnp.concatenate([scaled_t, reach_t], axis=0)), split(inverse)))
    ends = jnp.concatenate([eye, keys_wide], axis=0) - mm3(solved2, unit2)
    own_seg[...] = ends.astype(BF16)

    seg_swap = pltpu.make_async_remote_copy(
        own_seg, sib_seg, pair_send.at[3], pair_recv.at[3], device_id=sibling, device_id_type=MESH
    )
    seg_swap.start()
    seg_swap.wait_recv()
    first = c == 0
    own_hop, own_keys = own_seg[0:width, :], own_seg[width : width + tokens, :]
    sib_hop, sib_keys = sib_seg[0:width, :], sib_seg[width : width + tokens, :]
    moved = jnp.where(first, mm(own_keys, sib_hop), own_keys.astype(F32))
    hops = jnp.where(first, mm(own_hop, sib_hop), mm(sib_hop, own_hop))
    hops = jnp.where(first, hops[0:half, :], hops[half:, :])
    quarter = half // 2
    for side in range(2):
        own_part = jnp.concatenate([moved[side * part : (side + 1) * part, :], hops[side * quarter : (side + 1) * quarter, :]], axis=0)
        key[0, pl.ds(c, 1), side] = own_part.astype(BF16)[None]
    forward_relays(KEY, 0, begin)

    pl.when(z <= 1)(lambda: pl.semaphore_wait(ready.at[3], 1))
    pl.when(z == 0)(lambda: pl.semaphore_wait(ready.at[2], 1))
    backward_relays(VAL, 0, begin)
    backward_relays(KEY, 0, begin)

    line_stage(VAL, 0)

    loads[5].wait()
    for head in range(heads):
        q_rows[head * tokens : (head + 1) * tokens, :] = q_own[:, head * width : (head + 1) * width]
    unit_t2 = split(unit_t)
    q = q_rows[...]
    products = mm(q, jnp.concatenate([unit_t2[0], unit_t2[1], keys_t], axis=1))
    causal = jnp.concatenate([rows_i >= cols_i] * heads, axis=0)
    onto = products[:, 0:tokens] + products[:, tokens : 2 * tokens]
    taken = mm3(split(jnp.where(causal, onto, 0.0)), solved2, NT)
    q_rows[...] = (q.astype(F32) - taken[:, 0:width]).astype(BF16)
    scores = (products[:, 2 * tokens :] - taken[:, width:]) * factor
    scores = jnp.where(causal, scores, LOW)
    top = jnp.max(scores, axis=1, keepdims=True)
    weights = jnp.exp2(scores - top)
    peak[...] = jnp.broadcast_to(top, peak.shape)
    total[...] = weights
    acc[...] = mm(weights.astype(BF16), values_own)

    def absorb(key_block, value_block, mask):
        scores = mask(mm(q_rows[...], key_block(), NT))
        old = peak[...]
        top = jnp.maximum(old, jnp.max(scores, axis=1, keepdims=True))
        fade = jnp.exp2(old - top)
        peak[...] = top
        parts = []
        sums = total[...] * fade
        for i in range(scores.shape[1] // width):
            weights = jnp.exp2(scores[:, i * width : (i + 1) * width] - top)
            sums = sums + weights
            parts.append(weights.astype(BF16))
        total[...] = sums
        both = jnp.concatenate(parts, axis=1) if len(parts) > 1 else parts[0]
        acc[...] = acc[...] * fade + mm(both, value_block())

    near_arrival(VAL, 0).wait_recv()

    @pl.when(c == 1)
    def _():
        keys_now[0:tokens, :] = (sib_seg[width : width + tokens, :].astype(F32) * factor).astype(BF16)
        absorb(lambda: keys_now[0:tokens, :], lambda: val[0, 0].reshape(tokens, width), lambda x: x)

    chain[...] = jnp.where(first, eye, sib_seg[0:width, :].astype(F32)).astype(BF16)

    block = 2 * tokens

    def hop_of(d):
        return key[d, :, :, part:, :].reshape(width, width)

    def keys_of(d):
        return key[d, :, :, 0:part, :].reshape(block, width)

    def carry(j, d):
        now = chain[...]
        keys_now[j * block : (j + 1) * block, :] = (mm(keys_of(d), now) * factor).astype(BF16)
        chain[...] = mm(hop_of(d), now).astype(BF16)

    def await_block(d, kinds=(KEY, VAL)):
        for kind in kinds:
            near_arrival(kind, d).wait_recv()

    def masked(first_block):
        def mask(scores):
            return jnp.concatenate(
                [
                    jnp.where(z >= first_block + j, scores[:, j * block : (j + 1) * block], LOW)
                    for j in range(scores.shape[1] // block)
                ],
                axis=1,
            )

        return mask

    @pl.loop(0, reach // 2)
    def _(i):
        m = i - 1
        line_stage(KEY, i)

        @pl.when(2 * i + 2 < reach)
        def _():
            line_stage(VAL, i + 1)

        @pl.when(i >= 1)
        def _():
            cross_stage(KEY, m)
            cross_stage(VAL, m)

        @pl.when((i >= 1) & (z >= 2 * m + 1))
        def _():
            d1, d2 = 2 * m + 1, 2 * m + 2
            await_block(d1)
            pl.when(z >= d2)(lambda: await_block(d2))
            carry(0, d1)
            carry(1, d2)
            absorb(
                lambda: keys_now[0 : 2 * block, :],
                lambda: val[pl.ds(d1, 2)].reshape(2 * block, width),
                masked(d1),
            )

    tail, beyond = reach - 1, reach + 2

    @pl.when(z >= beyond)
    def _():
        for d in range(beyond, chips):
            pl.when(z >= d)(lambda d=d: await_block(d))
        so_far = None
        for d in range(beyond, chips):
            at = (d - beyond) * block
            if so_far is None:
                far_keys[at : at + block, :] = keys_of(d)
                so_far = hop_of(d)
            else:
                far_keys[at : at + block, :] = mm(keys_of(d), so_far).astype(BF16)
                so_far = mm(hop_of(d), so_far).astype(BF16)

    cross_stage(KEY, reach // 2 - 1)
    cross_stage(VAL, reach // 2 - 1)

    @pl.when(z >= tail)
    def _():
        for d in (tail, tail + 1, tail + 2):
            pl.when(z >= d)(lambda d=d: await_block(d))
        for j, d in enumerate((tail, tail + 1, tail + 2)):
            carry(j, d)
        absorb(
            lambda: keys_now[...],
            lambda: val[tail : tail + 3].reshape(3 * block, width),
            masked(tail),
        )

    @pl.when(z >= beyond)
    def _():
        far_keys[...] = (mm(far_keys[...], chain[...]) * factor).astype(BF16)
        absorb(
            lambda: far_keys[...],
            lambda: val[beyond:chips].reshape((chips - beyond) * block, width),
            masked(beyond),
        )

    loads[4].wait()
    gain = gain_own[...]
    for head in range(heads):
        span = slice(head * tokens, (head + 1) * tokens)
        mixed = acc[span, :] / jnp.sum(total[span, :], axis=1, keepdims=True)
        strength = lax.rsqrt(jnp.mean(mixed * mixed, axis=1, keepdims=True) + 1e-06)
        o_ref[:, head * width : (head + 1) * width] = (mixed * strength * gain).astype(BF16)

    def left(copy):
        copy.wait_send()

    for copy in swaps:
        copy.wait_send()
    seg_swap.wait_send()
    near_copy(VAL, 0).wait_send()

    for kind in (KEY, VAL):

        @pl.loop(0, reach // 2)
        def _(m, kind=kind):
            forward_relays(kind, 2 * m, left)
            backward_relays(kind, 2 * m, left)

    @pl.loop(1, chips)
    def _(d):
        @pl.when(z >= d)
        def _():
            for kind in (KEY, VAL):
                near_copy(kind, d).wait_send()
            for kind in (KEY, VAL):
                cross_copy(kind, d, parity).wait_send()


def solution(mesh):
    chips = mesh.shape["seq"] // 2

    def step(q, k, v, u, beta, gain):
        tokens, width = k.shape[0], 2 * k.shape[1]
        rows = tokens * (q.shape[1] // width)
        slots = chips + 1
        return pl.pallas_call(
            functools.partial(kernel, chips),
            out_shape=jax.ShapeDtypeStruct(q.shape, BF16),
            in_specs=[pl.BlockSpec(memory_space=pltpu.HBM)] * 6,
            out_specs=pl.BlockSpec(memory_space=pltpu.VMEM),
            scratch_shapes=[
                pltpu.VMEM(q.shape, BF16),
                pltpu.VMEM((3, width, tokens), BF16),
                pltpu.VMEM((beta.shape[1], tokens), F32),
                pltpu.VMEM((1, width), F32),
                pltpu.VMEM((width + tokens, width), BF16),
                pltpu.VMEM((width + tokens, width), BF16),
                pltpu.VMEM((slots, 2, 2, tokens // 2 + width // 4, width), BF16),
                pltpu.VMEM((slots, 2, 2, tokens // 2, width), BF16),
                pltpu.VMEM((rows, width), BF16),
                pltpu.VMEM((rows, width), F32),
                pltpu.VMEM((rows, width), F32),
                pltpu.VMEM((rows, width), F32),
                pltpu.VMEM((width, width), BF16),
                pltpu.VMEM((6 * tokens, width), BF16),
                pltpu.VMEM(((chips - chips // 2 - 2) * 2 * tokens, width), BF16),
                pltpu.SemaphoreType.DMA((6,)),
                pltpu.SemaphoreType.DMA((4,)),
                pltpu.SemaphoreType.DMA((4,)),
                pltpu.SemaphoreType.DMA((2, slots)),
                pltpu.SemaphoreType.DMA((2, slots)),
                pltpu.SemaphoreType.DMA((2, slots)),
                pltpu.SemaphoreType.DMA((2, slots)),
                pltpu.SemaphoreType.DMA((2, slots)),
                pltpu.SemaphoreType.DMA((2, slots)),
                pltpu.SemaphoreType.REGULAR((4,)),
            ],
            compiler_params=pltpu.CompilerParams(
                collective_id=0, has_side_effects=True, vmem_limit_bytes=60 * 2**20
            ),
        )(q, k.T, v.T, u.T, beta.T, gain.reshape(1, width))

    return jax.shard_map(
        step,
        mesh=mesh,
        in_specs=(P("seq", "head"),) * 4 + (P("seq", None), P()),
        out_specs=P("seq", "head"),
        check_vma=False,
    )
```

```python
import functools
import math

import jax
import jax.numpy as jnp
from jax import lax
from jax.experimental import pallas as pl
from jax.experimental.pallas import tpu as pltpu
from jax.sharding import PartitionSpec as P

MESH = pl.DeviceIdType.MESH
F32 = jnp.float32
BF16 = jnp.bfloat16
NN = (((1,), (0,)), ((), ()))
NT = (((1,), (1,)), ((), ()))
LOW = -1e30
KEY, VAL = 0, 1


def mm(a, b, dims=NN):
    return lax.dot_general(a, b, dims, preferred_element_type=F32)


def split(x):
    high = x.astype(BF16)
    return high, (x - high.astype(F32)).astype(BF16)


def mm3(a, b, dims=NN):
    return mm(a[0], b[0], dims) + (mm(a[0], b[1], dims) + mm(a[1], b[0], dims))


def kernel(
    chips, q_ref, k_ref, v_ref, u_ref, beta_ref, gain_ref, o_ref,
    q_own, whole, beta_own, gain_own, own_seg, sib_seg, key, val, q_rows, peak, total, acc, chain, keys_now, far_keys,
    local, pair_send, pair_recv, line_send, line_recv, near_send, near_recv, cross_send, cross_recv, ready,
):
    half, tokens = k_ref.shape
    width = 2 * half
    heads = q_ref.shape[1] // width
    factor = math.log2(math.e) / math.sqrt(width)
    s, h = lax.axis_index("seq"), lax.axis_index("head")
    z, c = lax.div(s, 2), lax.rem(s, 2)
    last = chips - 1

    def chip(place):
        return (place * 2 + c, h)

    partner = (s, h + 1 - 2 * lax.rem(h, 2))
    sibling = (s + 1 - 2 * c, h)

    parity = lax.rem(h, 2)
    own_rows = pl.ds(parity * half, half)
    halves = (u_ref, k_ref, v_ref)
    loads = [
        pltpu.make_async_copy(src, dst, local.at[i])
        for i, (src, dst) in enumerate(
            [(src, whole.at[i, own_rows]) for i, src in enumerate(halves)]
            + [(beta_ref, beta_own), (gain_ref, gain_own), (q_ref, q_own)]
        )
    ]
    for copy in loads:
        copy.start()

    barrier = pltpu.get_barrier_semaphore()

    def tell(sem, device):
        pl.semaphore_signal(sem, inc=1, device_id=device, device_id_type=MESH)

    tell(barrier, partner)
    tell(barrier, sibling)
    pl.when(z + 1 <= last)(lambda: tell(barrier, chip(z + 1)))
    pl.when(z + 2 <= last)(lambda: tell(barrier, chip(z + 2)))
    pl.when(z <= 1)(lambda: tell(barrier, chip(last)))
    pl.when(z == 0)(lambda: tell(barrier, chip(last - 1)))
    extra = jnp.where(z == last, 2, jnp.where(z == last - 1, 1, 0))
    pl.semaphore_wait(barrier, 2 + jnp.minimum(z, 2) + extra)
    pl.when(z >= 1)(lambda: tell(ready.at[0], chip(z - 1)))
    pl.when(z >= 2)(lambda: tell(ready.at[1], chip(z - 2)))
    pl.when(z == last)(lambda: tell(ready.at[2], chip(0)))
    pl.when(z == last)(lambda: tell(ready.at[3], chip(1)))
    pl.when(z == last - 1)(lambda: tell(ready.at[3], chip(0)))

    swaps = [
        pltpu.make_async_remote_copy(
            src, whole.at[i, own_rows], pair_send.at[i], pair_recv.at[i],
            device_id=partner, device_id_type=MESH,
        )
        for i, src in enumerate(halves)
    ]
    for copy in swaps:
        copy.start()

    rows_i = lax.broadcasted_iota(jnp.int32, (tokens, tokens), 0)
    cols_i = lax.broadcasted_iota(jnp.int32, (tokens, tokens), 1)
    eye = (rows_i == cols_i).astype(F32)

    def swapped(i):
        rows = pl.ds((1 - parity) * half, half)
        loads[i].wait()
        pltpu.make_async_remote_copy(
            halves[i], whole.at[i, rows], pair_send.at[i], pair_recv.at[i],
            device_id=partner, device_id_type=MESH,
        ).wait_recv()
        return whole[i]

    buffers = (key, val)

    def line_copy(kind, source_slot, target_slot, device):
        return pltpu.make_async_remote_copy(
            buffers[kind].at[source_slot, c, parity],
            buffers[kind].at[target_slot, c, parity],
            line_send.at[kind, target_slot],
            line_recv.at[kind, target_slot],
            device_id=device,
            device_id_type=MESH,
        )

    part = tokens // 2

    def near_piece(kind, slot, core):
        return buffers[kind].at[slot, core]

    def near_transfer(kind, slot, core):
        return pltpu.make_async_remote_copy(
            near_piece(kind, slot, core),
            near_piece(kind, slot, core),
            near_send.at[kind, slot],
            near_recv.at[kind, slot],
            device_id=sibling,
            device_id_type=MESH,
        )

    def near_copy(kind, slot):
        return near_transfer(kind, slot, c)

    def near_arrival(kind, slot):
        return near_transfer(kind, slot, 1 - c)

    def cross_copy(kind, slot, side):
        return pltpu.make_async_remote_copy(
            buffers[kind].at[slot, c, side],
            buffers[kind].at[slot, c, side],
            cross_send.at[kind, slot],
            cross_recv.at[kind, slot],
            device_id=partner,
            device_id_type=MESH,
        )

    reach = chips // 2
    far = chips - reach - 1

    def forward_relays(kind, d, act):
        @pl.when((z >= d) & (d + 1 <= reach) & (z + 1 <= last))
        def _():
            act(line_copy(kind, d, d + 1, chip(z + 1)))

        @pl.when((z >= d) & (d + 2 <= reach) & (z + 2 <= last))
        def _():
            act(line_copy(kind, d, d + 2, chip(z + 2)))

    def backward_relays(kind, e, act):
        slot = lax.rem(chips - e, chips)
        wrapped = z + e >= chips
        held = (z + e < far) | wrapped

        @pl.when(held & (wrapped | (z == 0)) & (e + 1 <= far))
        def _():
            act(line_copy(kind, slot, chips - e - 1, chip(lax.rem(z + chips - 1, chips))))

        @pl.when(held & (e + 2 < far))
        def _():
            act(line_copy(kind, slot, chips - e - 2, chip(lax.rem(z + chips - 2, chips))))

    def begin(copy):
        copy.start()

    def arrive(kind, slot):
        line_copy(kind, slot, slot, sibling).wait_recv()

    def spread(kind, slot):
        cross_copy(kind, slot, parity).start()

    def line_stage(kind, m):
        d1, d2 = 2 * m + 1, 2 * m + 2
        pl.when(z >= d2)(lambda: arrive(kind, d2))
        forward_relays(kind, d2, begin)
        pl.when(z >= d2)(lambda: spread(kind, d2))

        @pl.when(z >= d1)
        def _():
            arrive(kind, d1)
            spread(kind, d1)

        @pl.when((d2 < far) & ((z + d2 < far) | (z + d2 >= chips)))
        def _():
            arrive(kind, chips - d2)

        @pl.when(d2 < far)
        def _():
            backward_relays(kind, d2, begin)

        @pl.when((d2 < far) & (z + d2 >= chips))
        def _():
            spread(kind, chips - d2)

        @pl.when((d1 <= far) & (z + d1 >= chips))
        def _():
            arrive(kind, chips - d1)
            spread(kind, chips - d1)

    def cross_stage(kind, m):
        d1, d2 = 2 * m + 1, 2 * m + 2

        def take(slot):
            cross_copy(kind, slot, 1 - parity).wait_recv()
            near_copy(kind, slot).start()

        pl.when(z >= d1)(lambda: take(d1))
        pl.when(z >= d2)(lambda: take(d2))
        pl.when((d2 < far) & (z + d2 >= chips))(lambda: take(chips - d2))
        pl.when((d1 <= far) & (z + d1 >= chips))(lambda: take(chips - d1))

    def clear(slot):
        for buffer in buffers:
            buffer[pl.ds(slot, 1)] = jnp.zeros((1,) + buffer.shape[1:], BF16)

    pl.when((lax.rem(z, 2) == 1) & (z < reach - 1))(lambda: clear(z + 1))

    @pl.when(z >= reach - 1)
    def _():
        @pl.loop(z + 1, chips)
        def _(slot):
            clear(slot)

    loads[3].wait()
    lane = lax.broadcasted_iota(jnp.int32, beta_ref.shape, 0)
    beta = jnp.sum(jnp.where(lane == lax.div(h, 2), beta_own[...], 0.0), axis=0, keepdims=True)
    raw_t = swapped(0).astype(F32)
    unit_t = raw_t * lax.rsqrt(jnp.sum(raw_t * raw_t, axis=0, keepdims=True) + 1e-06)
    scaled_t = beta * unit_t
    unit2, scaled_t2 = split(jnp.transpose(unit_t)), split(scaled_t)
    upper = cols_i > rows_i
    nil_t = jnp.where(upper, mm3(unit2, scaled_t2), 0.0)
    keys_t = swapped(1)
    keys_wide = jnp.transpose(keys_t.astype(F32))
    keys_own = keys_wide.astype(BF16)
    reach_t = jnp.where(upper, mm(keys_own, scaled_t2[0]) + mm(keys_own, scaled_t2[1]), 0.0)
    values_own = jnp.transpose(swapped(2).astype(F32)).astype(BF16)
    val[0, pl.ds(c, 1)] = values_own.reshape((1,) + val.shape[2:])
    near_copy(VAL, 0).start()

    pl.when(z + 1 <= last)(lambda: pl.semaphore_wait(ready.at[0], 1))
    pl.when(z + 2 <= last)(lambda: pl.semaphore_wait(ready.at[1], 1))
    forward_relays(VAL, 0, begin)

    inverse = eye
    size = 1
    while size < tokens:
        bits = size.bit_length() - 1
        block_r, block_c = rows_i >> bits, cols_i >> bits
        corner = jnp.where(((block_c & 1) == 1) & (block_r == block_c - 1), nil_t, 0.0)
        if size == 1:
            inverse = eye - corner
        else:
            inv2 = split(inverse)
            inverse = inverse - mm3(split(mm3(inv2, split(corner))), inv2)
        size *= 2
    solved2 = split(mm3(split(jnp.concatenate([scaled_t, reach_t], axis=0)), split(inverse)))
    ends = jnp.concatenate([eye, keys_wide], axis=0) - mm3(solved2, unit2)
    own_seg[...] = ends.astype(BF16)

    seg_swap = pltpu.make_async_remote_copy(
        own_seg, sib_seg, pair_send.at[3], pair_recv.at[3], device_id=sibling, device_id_type=MESH
    )
    seg_swap.start()
    seg_swap.wait_recv()
    first = c == 0
    own_hop, own_keys = own_seg[0:width, :], own_seg[width : width + tokens, :]
    sib_hop, sib_keys = sib_seg[0:width, :], sib_seg[width : width + tokens, :]
    moved = jnp.where(first, mm(own_keys, sib_hop), own_keys.astype(F32))
    hops = jnp.where(first, mm(own_hop, sib_hop), mm(sib_hop, own_hop))
    hops = jnp.where(first, hops[0:half, :], hops[half:, :])
    quarter = half // 2
    for side in range(2):
        own_part = jnp.concatenate([moved[side * part : (side + 1) * part, :], hops[side * quarter : (side + 1) * quarter, :]], axis=0)
        key[0, pl.ds(c, 1), side] = own_part.astype(BF16)[None]
    forward_relays(KEY, 0, begin)

    pl.when(z <= 1)(lambda: pl.semaphore_wait(ready.at[3], 1))
    pl.when(z == 0)(lambda: pl.semaphore_wait(ready.at[2], 1))
    backward_relays(VAL, 0, begin)
    backward_relays(KEY, 0, begin)

    line_stage(VAL, 0)

    loads[5].wait()
    for head in range(heads):
        q_rows[head * tokens : (head + 1) * tokens, :] = q_own[:, head * width : (head + 1) * width]
    unit_t2 = split(unit_t)
    q = q_rows[...]
    products = mm(q, jnp.concatenate([unit_t2[0], unit_t2[1], keys_t], axis=1))
    causal = jnp.concatenate([rows_i >= cols_i] * heads, axis=0)
    onto = products[:, 0:tokens] + products[:, tokens : 2 * tokens]
    taken = mm3(split(jnp.where(causal, onto, 0.0)), solved2, NT)
    q_rows[...] = (q.astype(F32) - taken[:, 0:width]).astype(BF16)
    scores = (products[:, 2 * tokens :] - taken[:, width:]) * factor
    scores = jnp.where(causal, scores, LOW)
    top = jnp.max(scores, axis=1, keepdims=True)
    weights = jnp.exp2(scores - top)
    peak[...] = jnp.broadcast_to(top, peak.shape)
    total[...] = weights
    acc[...] = mm(weights.astype(BF16), values_own)

    def absorb(key_block, value_block, mask):
        scores = mask(mm(q_rows[...], key_block(), NT))
        old = peak[...]
        top = jnp.maximum(old, jnp.max(scores, axis=1, keepdims=True))
        fade = jnp.exp2(old - top)
        peak[...] = top
        parts = []
        sums = total[...] * fade
        for i in range(scores.shape[1] // width):
            weights = jnp.exp2(scores[:, i * width : (i + 1) * width] - top)
            sums = sums + weights
            parts.append(weights.astype(BF16))
        total[...] = sums
        both = jnp.concatenate(parts, axis=1) if len(parts) > 1 else parts[0]
        acc[...] = acc[...] * fade + mm(both, value_block())

    near_arrival(VAL, 0).wait_recv()

    @pl.when(c == 1)
    def _():
        keys_now[0:tokens, :] = (sib_seg[width : width + tokens, :].astype(F32) * factor).astype(BF16)
        absorb(lambda: keys_now[0:tokens, :], lambda: val[0, 0].reshape(tokens, width), lambda x: x)

    chain[...] = jnp.where(first, eye, sib_seg[0:width, :].astype(F32)).astype(BF16)

    block = 2 * tokens

    def hop_of(d):
        return key[d, :, :, part:, :].reshape(width, width)

    def keys_of(d):
        return key[d, :, :, 0:part, :].reshape(block, width)

    def carry(j, d):
        now = chain[...]
        keys_now[j * block : (j + 1) * block, :] = (mm(keys_of(d), now) * factor).astype(BF16)
        chain[...] = mm(hop_of(d), now).astype(BF16)

    def await_block(d, kinds=(KEY, VAL)):
        for kind in kinds:
            near_arrival(kind, d).wait_recv()

    def masked(first_block):
        def mask(scores):
            return jnp.concatenate(
                [
                    jnp.where(z >= first_block + j, scores[:, j * block : (j + 1) * block], LOW)
                    for j in range(scores.shape[1] // block)
                ],
                axis=1,
            )

        return mask

    @pl.loop(0, reach // 2)
    def _(i):
        m = i - 1
        line_stage(KEY, i)

        @pl.when(i >= 1)
        def _():
            cross_stage(KEY, m)
            cross_stage(VAL, m)

        @pl.when(2 * i + 2 < reach)
        def _():
            line_stage(VAL, i + 1)

        @pl.when((i >= 1) & (z >= 2 * m + 1))
        def _():
            d1, d2 = 2 * m + 1, 2 * m + 2
            await_block(d1)
            pl.when(z >= d2)(lambda: await_block(d2))
            carry(0, d1)
            carry(1, d2)
            absorb(
                lambda: keys_now[0 : 2 * block, :],
                lambda: val[pl.ds(d1, 2)].reshape(2 * block, width),
                masked(d1),
            )

    tail, beyond = reach - 1, reach + 2

    @pl.when(z >= beyond)
    def _():
        for d in range(beyond, chips):
            pl.when(z >= d)(lambda d=d: await_block(d))
        so_far = None
        for d in range(beyond, chips):
            at = (d - beyond) * block
            if so_far is None:
                far_keys[at : at + block, :] = keys_of(d)
                so_far = hop_of(d)
            else:
                far_keys[at : at + block, :] = mm(keys_of(d), so_far).astype(BF16)
                so_far = mm(hop_of(d), so_far).astype(BF16)

    cross_stage(KEY, reach // 2 - 1)
    cross_stage(VAL, reach // 2 - 1)

    @pl.when(z >= tail)
    def _():
        for d in (tail, tail + 1, tail + 2):
            pl.when(z >= d)(lambda d=d: await_block(d))
        for j, d in enumerate((tail, tail + 1, tail + 2)):
            carry(j, d)
        absorb(
            lambda: keys_now[...],
            lambda: val[tail : tail + 3].reshape(3 * block, width),
            masked(tail),
        )

    @pl.when(z >= beyond)
    def _():
        far_keys[...] = (mm(far_keys[...], chain[...]) * factor).astype(BF16)
        absorb(
            lambda: far_keys[...],
            lambda: val[beyond:chips].reshape((chips - beyond) * block, width),
            masked(beyond),
        )

    loads[4].wait()
    gain = gain_own[...]
    for head in range(heads):
        span = slice(head * tokens, (head + 1) * tokens)
        mixed = acc[span, :] / jnp.sum(total[span, :], axis=1, keepdims=True)
        strength = lax.rsqrt(jnp.mean(mixed * mixed, axis=1, keepdims=True) + 1e-06)
        o_ref[:, head * width : (head + 1) * width] = (mixed * strength * gain).astype(BF16)

    def left(copy):
        copy.wait_send()

    for copy in swaps:
        copy.wait_send()
    seg_swap.wait_send()
    near_copy(VAL, 0).wait_send()

    for kind in (KEY, VAL):

        @pl.loop(0, reach // 2)
        def _(m, kind=kind):
            forward_relays(kind, 2 * m, left)
            backward_relays(kind, 2 * m, left)

    @pl.loop(1, chips)
    def _(d):
        @pl.when(z >= d)
        def _():
            for kind in (KEY, VAL):
                near_copy(kind, d).wait_send()
            for kind in (KEY, VAL):
                cross_copy(kind, d, parity).wait_send()


def solution(mesh):
    chips = mesh.shape["seq"] // 2

    def step(q, k, v, u, beta, gain):
        tokens, width = k.shape[0], 2 * k.shape[1]
        rows = tokens * (q.shape[1] // width)
        slots = chips + 1
        return pl.pallas_call(
            functools.partial(kernel, chips),
            out_shape=jax.ShapeDtypeStruct(q.shape, BF16),
            in_specs=[pl.BlockSpec(memory_space=pltpu.HBM)] * 6,
            out_specs=pl.BlockSpec(memory_space=pltpu.VMEM),
            scratch_shapes=[
                pltpu.VMEM(q.shape, BF16),
                pltpu.VMEM((3, width, tokens), BF16),
                pltpu.VMEM((beta.shape[1], tokens), F32),
                pltpu.VMEM((1, width), F32),
                pltpu.VMEM((width + tokens, width), BF16),
                pltpu.VMEM((width + tokens, width), BF16),
                pltpu.VMEM((slots, 2, 2, tokens // 2 + width // 4, width), BF16),
                pltpu.VMEM((slots, 2, 2, tokens // 2, width), BF16),
                pltpu.VMEM((rows, width), BF16),
                pltpu.VMEM((rows, width), F32),
                pltpu.VMEM((rows, width), F32),
                pltpu.VMEM((rows, width), F32),
                pltpu.VMEM((width, width), BF16),
                pltpu.VMEM((6 * tokens, width), BF16),
                pltpu.VMEM(((chips - chips // 2 - 2) * 2 * tokens, width), BF16),
                pltpu.SemaphoreType.DMA((6,)),
                pltpu.SemaphoreType.DMA((4,)),
                pltpu.SemaphoreType.DMA((4,)),
                pltpu.SemaphoreType.DMA((2, slots)),
                pltpu.SemaphoreType.DMA((2, slots)),
                pltpu.SemaphoreType.DMA((2, slots)),
                pltpu.SemaphoreType.DMA((2, slots)),
                pltpu.SemaphoreType.DMA((2, slots)),
                pltpu.SemaphoreType.DMA((2, slots)),
                pltpu.SemaphoreType.REGULAR((4,)),
            ],
            compiler_params=pltpu.CompilerParams(
                collective_id=0, has_side_effects=True, vmem_limit_bytes=60 * 2**20
            ),
        )(q, k.T, v.T, u.T, beta.T, gain.reshape(1, width))

    return jax.shard_map(
        step,
        mesh=mesh,
        in_specs=(P("seq", "head"),) * 4 + (P("seq", None), P()),
        out_specs=P("seq", "head"),
        check_vma=False,
    )
```

```python
import functools
import math

import jax
import jax.numpy as jnp
from jax import lax
from jax.experimental import pallas as pl
from jax.experimental.pallas import tpu as pltpu
from jax.sharding import PartitionSpec as P

MESH = pl.DeviceIdType.MESH
F32 = jnp.float32
BF16 = jnp.bfloat16
NN = (((1,), (0,)), ((), ()))
NT = (((1,), (1,)), ((), ()))
LOW = -1e30
KEY, VAL = 0, 1


def mm(a, b, dims=NN):
    return lax.dot_general(a, b, dims, preferred_element_type=F32)


def split(x):
    high = x.astype(BF16)
    return high, (x - high.astype(F32)).astype(BF16)


def mm3(a, b, dims=NN):
    return mm(a[0], b[0], dims) + (mm(a[0], b[1], dims) + mm(a[1], b[0], dims))


def kernel(
    chips, q_ref, k_ref, v_ref, u_ref, beta_ref, gain_ref, o_ref,
    q_own, whole, beta_own, gain_own, own_seg, sib_seg, key, val, q_rows, peak, total, acc, chain, keys_now,
    local, pair_send, pair_recv, line_send, line_recv, near_send, near_recv, cross_send, cross_recv, ready,
):
    half, tokens = k_ref.shape
    width = 2 * half
    heads = q_ref.shape[1] // width
    factor = math.log2(math.e) / math.sqrt(width)
    s, h = lax.axis_index("seq"), lax.axis_index("head")
    z, c = lax.div(s, 2), lax.rem(s, 2)
    last = chips - 1

    def chip(place):
        return (place * 2 + c, h)

    partner = (s, h + 1 - 2 * lax.rem(h, 2))
    sibling = (s + 1 - 2 * c, h)

    parity = lax.rem(h, 2)
    own_rows = pl.ds(parity * half, half)
    halves = (u_ref, k_ref, v_ref)
    loads = [
        pltpu.make_async_copy(src, dst, local.at[i])
        for i, (src, dst) in enumerate(
            [(src, whole.at[i, own_rows]) for i, src in enumerate(halves)]
            + [(beta_ref, beta_own), (gain_ref, gain_own), (q_ref, q_own)]
        )
    ]
    for copy in loads:
        copy.start()

    barrier = pltpu.get_barrier_semaphore()

    def tell(sem, device):
        pl.semaphore_signal(sem, inc=1, device_id=device, device_id_type=MESH)

    tell(barrier, partner)
    tell(barrier, sibling)
    pl.when(z + 1 <= last)(lambda: tell(barrier, chip(z + 1)))
    pl.when(z + 2 <= last)(lambda: tell(barrier, chip(z + 2)))
    pl.when(z <= 1)(lambda: tell(barrier, chip(last)))
    pl.when(z == 0)(lambda: tell(barrier, chip(last - 1)))
    extra = jnp.where(z == last, 2, jnp.where(z == last - 1, 1, 0))
    pl.semaphore_wait(barrier, 2 + jnp.minimum(z, 2) + extra)
    pl.when(z >= 1)(lambda: tell(ready.at[0], chip(z - 1)))
    pl.when(z >= 2)(lambda: tell(ready.at[1], chip(z - 2)))
    pl.when(z == last)(lambda: tell(ready.at[2], chip(0)))
    pl.when(z == last)(lambda: tell(ready.at[3], chip(1)))
    pl.when(z == last - 1)(lambda: tell(ready.at[3], chip(0)))

    swaps = [
        pltpu.make_async_remote_copy(
            src, whole.at[i, own_rows], pair_send.at[i], pair_recv.at[i],
            device_id=partner, device_id_type=MESH,
        )
        for i, src in enumerate(halves)
    ]
    for copy in swaps:
        copy.start()

    rows_i = lax.broadcasted_iota(jnp.int32, (tokens, tokens), 0)
    cols_i = lax.broadcasted_iota(jnp.int32, (tokens, tokens), 1)
    eye = (rows_i == cols_i).astype(F32)

    def swapped(i):
        rows = pl.ds((1 - parity) * half, half)
        loads[i].wait()
        pltpu.make_async_remote_copy(
            halves[i], whole.at[i, rows], pair_send.at[i], pair_recv.at[i],
            device_id=partner, device_id_type=MESH,
        ).wait_recv()
        return whole[i]

    buffers = (key, val)

    def line_copy(kind, source_slot, target_slot, device):
        return pltpu.make_async_remote_copy(
            buffers[kind].at[source_slot, c, parity],
            buffers[kind].at[target_slot, c, parity],
            line_send.at[kind, target_slot],
            line_recv.at[kind, target_slot],
            device_id=device,
            device_id_type=MESH,
        )

    part = tokens // 2

    def near_piece(kind, slot, core):
        return buffers[kind].at[slot, core]

    def near_transfer(kind, slot, core):
        return pltpu.make_async_remote_copy(
            near_piece(kind, slot, core),
            near_piece(kind, slot, core),
            near_send.at[kind, slot],
            near_recv.at[kind, slot],
            device_id=sibling,
            device_id_type=MESH,
        )

    def near_copy(kind, slot):
        return near_transfer(kind, slot, c)

    def near_arrival(kind, slot):
        return near_transfer(kind, slot, 1 - c)

    def cross_copy(kind, slot, side):
        return pltpu.make_async_remote_copy(
            buffers[kind].at[slot, c, side],
            buffers[kind].at[slot, c, side],
            cross_send.at[kind, slot],
            cross_recv.at[kind, slot],
            device_id=partner,
            device_id_type=MESH,
        )

    reach = chips // 2
    far = chips - reach - 1

    def forward_relays(kind, d, act):
        @pl.when((z >= d) & (d + 1 <= reach) & (z + 1 <= last))
        def _():
            act(line_copy(kind, d, d + 1, chip(z + 1)))

        @pl.when((z >= d) & (d + 2 <= reach) & (z + 2 <= last))
        def _():
            act(line_copy(kind, d, d + 2, chip(z + 2)))

    def backward_relays(kind, e, act):
        slot = lax.rem(chips - e, chips)
        wrapped = z + e >= chips
        held = (z + e < far) | wrapped

        @pl.when(held & (wrapped | (z == 0)) & (e + 1 <= far))
        def _():
            act(line_copy(kind, slot, chips - e - 1, chip(lax.rem(z + chips - 1, chips))))

        @pl.when(held & (e + 2 < far))
        def _():
            act(line_copy(kind, slot, chips - e - 2, chip(lax.rem(z + chips - 2, chips))))

    def begin(copy):
        copy.start()

    def arrive(kind, slot):
        line_copy(kind, slot, slot, sibling).wait_recv()

    def spread(kind, slot):
        cross_copy(kind, slot, parity).start()

    def line_stage(kind, m):
        d1, d2 = 2 * m + 1, 2 * m + 2
        pl.when(z >= d2)(lambda: arrive(kind, d2))
        forward_relays(kind, d2, begin)
        pl.when(z >= d2)(lambda: spread(kind, d2))

        @pl.when(z >= d1)
        def _():
            arrive(kind, d1)
            spread(kind, d1)

        @pl.when((d2 < far) & ((z + d2 < far) | (z + d2 >= chips)))
        def _():
            arrive(kind, chips - d2)

        @pl.when(d2 < far)
        def _():
            backward_relays(kind, d2, begin)

        @pl.when((d2 < far) & (z + d2 >= chips))
        def _():
            spread(kind, chips - d2)

        @pl.when((d1 <= far) & (z + d1 >= chips))
        def _():
            arrive(kind, chips - d1)
            spread(kind, chips - d1)

    def cross_stage(kind, m):
        d1, d2 = 2 * m + 1, 2 * m + 2

        def take(slot):
            cross_copy(kind, slot, 1 - parity).wait_recv()
            near_copy(kind, slot).start()

        pl.when(z >= d1)(lambda: take(d1))
        pl.when(z >= d2)(lambda: take(d2))
        pl.when((d2 < far) & (z + d2 >= chips))(lambda: take(chips - d2))
        pl.when((d1 <= far) & (z + d1 >= chips))(lambda: take(chips - d1))

    def clear(slot):
        for buffer in buffers:
            buffer[pl.ds(slot, 1)] = jnp.zeros((1,) + buffer.shape[1:], BF16)

    pl.when((lax.rem(z, 2) == 1) & (z < reach - 1))(lambda: clear(z + 1))

    @pl.when(z >= reach - 1)
    def _():
        @pl.loop(z + 1, chips)
        def _(slot):
            clear(slot)

    loads[3].wait()
    lane = lax.broadcasted_iota(jnp.int32, beta_ref.shape, 0)
    beta = jnp.sum(jnp.where(lane == lax.div(h, 2), beta_own[...], 0.0), axis=0, keepdims=True)
    raw_t = swapped(0).astype(F32)
    unit_t = raw_t * lax.rsqrt(jnp.sum(raw_t * raw_t, axis=0, keepdims=True) + 1e-06)
    scaled_t = beta * unit_t
    unit2, scaled_t2 = split(jnp.transpose(unit_t)), split(scaled_t)
    upper = cols_i > rows_i
    nil_t = jnp.where(upper, mm3(unit2, scaled_t2), 0.0)
    keys_t = swapped(1)
    keys_wide = jnp.transpose(keys_t.astype(F32))
    keys_own = keys_wide.astype(BF16)
    reach_t = jnp.where(upper, mm(keys_own, scaled_t2[0]) + mm(keys_own, scaled_t2[1]), 0.0)
    values_own = jnp.transpose(swapped(2).astype(F32)).astype(BF16)
    val[0, pl.ds(c, 1)] = values_own.reshape((1,) + val.shape[2:])
    near_copy(VAL, 0).start()

    pl.when(z + 1 <= last)(lambda: pl.semaphore_wait(ready.at[0], 1))
    pl.when(z + 2 <= last)(lambda: pl.semaphore_wait(ready.at[1], 1))
    forward_relays(VAL, 0, begin)

    inverse = eye
    size = 1
    while size < tokens:
        bits = size.bit_length() - 1
        block_r, block_c = rows_i >> bits, cols_i >> bits
        corner = jnp.where(((block_c & 1) == 1) & (block_r == block_c - 1), nil_t, 0.0)
        if size == 1:
            inverse = eye - corner
        else:
            inv2 = split(inverse)
            inverse = inverse - mm3(split(mm3(inv2, split(corner))), inv2)
        size *= 2
    solved2 = split(mm3(split(jnp.concatenate([scaled_t, reach_t], axis=0)), split(inverse)))
    ends = jnp.concatenate([eye, keys_wide], axis=0) - mm3(solved2, unit2)
    own_seg[...] = ends.astype(BF16)

    seg_swap = pltpu.make_async_remote_copy(
        own_seg, sib_seg, pair_send.at[3], pair_recv.at[3], device_id=sibling, device_id_type=MESH
    )
    seg_swap.start()
    seg_swap.wait_recv()
    first = c == 0
    own_hop, own_keys = own_seg[0:width, :], own_seg[width : width + tokens, :]
    sib_hop, sib_keys = sib_seg[0:width, :], sib_seg[width : width + tokens, :]
    moved = jnp.where(first, mm(own_keys, sib_hop), own_keys.astype(F32))
    hops = jnp.where(first, mm(own_hop, sib_hop), mm(sib_hop, own_hop))
    hops = jnp.where(first, hops[0:half, :], hops[half:, :])
    quarter = half // 2
    for side in range(2):
        own_part = jnp.concatenate([moved[side * part : (side + 1) * part, :], hops[side * quarter : (side + 1) * quarter, :]], axis=0)
        key[0, pl.ds(c, 1), side] = own_part.astype(BF16)[None]
    forward_relays(KEY, 0, begin)

    pl.when(z <= 1)(lambda: pl.semaphore_wait(ready.at[3], 1))
    pl.when(z == 0)(lambda: pl.semaphore_wait(ready.at[2], 1))
    backward_relays(VAL, 0, begin)
    backward_relays(KEY, 0, begin)

    line_stage(VAL, 0)

    loads[5].wait()
    for head in range(heads):
        q_rows[head * tokens : (head + 1) * tokens, :] = q_own[:, head * width : (head + 1) * width]
    unit_t2 = split(unit_t)
    q = q_rows[...]
    products = mm(q, jnp.concatenate([unit_t2[0], unit_t2[1], keys_t], axis=1))
    causal = jnp.concatenate([rows_i >= cols_i] * heads, axis=0)
    onto = products[:, 0:tokens] + products[:, tokens : 2 * tokens]
    taken = mm3(split(jnp.where(causal, onto, 0.0)), solved2, NT)
    q_rows[...] = (q.astype(F32) - taken[:, 0:width]).astype(BF16)
    scores = (products[:, 2 * tokens :] - taken[:, width:]) * factor
    scores = jnp.where(causal, scores, LOW)
    top = jnp.max(scores, axis=1, keepdims=True)
    weights = jnp.exp2(scores - top)
    peak[...] = jnp.broadcast_to(top, peak.shape)
    total[...] = weights
    acc[...] = mm(weights.astype(BF16), values_own)

    def absorb(key_block, value_block, mask):
        scores = mask(mm(q_rows[...], key_block(), NT))
        old = peak[...]
        top = jnp.maximum(old, jnp.max(scores, axis=1, keepdims=True))
        fade = jnp.exp2(old - top)
        peak[...] = top
        parts = []
        sums = total[...] * fade
        for i in range(scores.shape[1] // width):
            weights = jnp.exp2(scores[:, i * width : (i + 1) * width] - top)
            sums = sums + weights
            parts.append(weights.astype(BF16))
        total[...] = sums
        both = jnp.concatenate(parts, axis=1) if len(parts) > 1 else parts[0]
        acc[...] = acc[...] * fade + mm(both, value_block())

    near_arrival(VAL, 0).wait_recv()

    @pl.when(c == 1)
    def _():
        keys_now[0:tokens, :] = (sib_seg[width : width + tokens, :].astype(F32) * factor).astype(BF16)
        absorb(lambda: keys_now[0:tokens, :], lambda: val[0, 0].reshape(tokens, width), lambda x: x)

    chain[...] = jnp.where(first, eye, sib_seg[0:width, :].astype(F32)).astype(BF16)

    block = 2 * tokens

    def hop_of(d):
        return key[d, :, :, part:, :].reshape(width, width)

    def keys_of(d):
        return key[d, :, :, 0:part, :].reshape(block, width)

    def carry(j, d):
        now = chain[...]
        keys_now[j * block : (j + 1) * block, :] = (mm(keys_of(d), now) * factor).astype(BF16)
        chain[...] = mm(hop_of(d), now).astype(BF16)

    def await_block(d, kinds=(KEY, VAL)):
        for kind in kinds:
            near_arrival(kind, d).wait_recv()

    def masked(first_block):
        def mask(scores):
            return jnp.concatenate(
                [
                    jnp.where(z >= first_block + j, scores[:, j * block : (j + 1) * block], LOW)
                    for j in range(scores.shape[1] // block)
                ],
                axis=1,
            )

        return mask

    @pl.loop(0, reach // 2)
    def _(i):
        m = i - 1
        line_stage(KEY, i)

        @pl.when(i >= 1)
        def _():
            cross_stage(KEY, m)
            cross_stage(VAL, m)

        @pl.when(2 * i + 2 < reach)
        def _():
            line_stage(VAL, i + 1)

        @pl.when((i >= 1) & (z >= 2 * m + 1))
        def _():
            d1, d2 = 2 * m + 1, 2 * m + 2
            await_block(d1)
            pl.when(z >= d2)(lambda: await_block(d2))
            carry(0, d1)
            carry(1, d2)
            absorb(
                lambda: keys_now[0 : 2 * block, :],
                lambda: val[pl.ds(d1, 2)].reshape(2 * block, width),
                masked(d1),
            )

    tail, beyond = reach - 1, reach + 2

    @pl.when(z >= beyond)
    def _():
        for d in range(beyond, chips):
            pl.when(z >= d)(lambda d=d: await_block(d))
        so_far = None
        for d in range(beyond, chips):
            at = (d - tail) * block
            if so_far is None:
                keys_now[at : at + block, :] = keys_of(d)
                so_far = hop_of(d)
            else:
                keys_now[at : at + block, :] = mm(keys_of(d), so_far).astype(BF16)
                so_far = mm(hop_of(d), so_far).astype(BF16)

    cross_stage(KEY, reach // 2 - 1)
    cross_stage(VAL, reach // 2 - 1)

    @pl.when(z >= tail)
    def _():
        for d in (tail, tail + 1, tail + 2):
            pl.when(z >= d)(lambda d=d: await_block(d))
        for j, d in enumerate((tail, tail + 1, tail + 2)):
            carry(j, d)

    def absorb_rest(count):
        absorb(
            lambda: keys_now[0 : count * block, :],
            lambda: val[tail : tail + count].reshape(count * block, width),
            masked(tail),
        )

    pl.when((z >= tail) & (z < beyond))(lambda: absorb_rest(3))

    @pl.when(z >= beyond)
    def _():
        keys_now[3 * block :, :] = (mm(keys_now[3 * block :, :], chain[...]) * factor).astype(BF16)
        absorb_rest(chips - tail)

    loads[4].wait()
    gain = gain_own[...]
    for head in range(heads):
        span = slice(head * tokens, (head + 1) * tokens)
        mixed = acc[span, :] * (1.0 / jnp.sum(total[span, :], axis=1, keepdims=True))
        strength = lax.rsqrt(jnp.mean(mixed * mixed, axis=1, keepdims=True) + 1e-06)
        o_ref[:, head * width : (head + 1) * width] = (mixed * strength * gain).astype(BF16)

    def left(copy):
        copy.wait_send()

    for copy in swaps:
        copy.wait_send()
    seg_swap.wait_send()
    near_copy(VAL, 0).wait_send()

    for kind in (KEY, VAL):

        @pl.loop(0, reach // 2)
        def _(m, kind=kind):
            forward_relays(kind, 2 * m, left)
            backward_relays(kind, 2 * m, left)

    @pl.loop(1, chips)
    def _(d):
        @pl.when(z >= d)
        def _():
            for kind in (KEY, VAL):
                near_copy(kind, d).wait_send()
            for kind in (KEY, VAL):
                cross_copy(kind, d, parity).wait_send()


def solution(mesh):
    chips = mesh.shape["seq"] // 2

    def step(q, k, v, u, beta, gain):
        tokens, width = k.shape[0], 2 * k.shape[1]
        rows = tokens * (q.shape[1] // width)
        slots = chips + 1
        return pl.pallas_call(
            functools.partial(kernel, chips),
            out_shape=jax.ShapeDtypeStruct(q.shape, BF16),
            in_specs=[pl.BlockSpec(memory_space=pltpu.HBM)] * 6,
            out_specs=pl.BlockSpec(memory_space=pltpu.VMEM),
            scratch_shapes=[
                pltpu.VMEM(q.shape, BF16),
                pltpu.VMEM((3, width, tokens), BF16),
                pltpu.VMEM((beta.shape[1], tokens), F32),
                pltpu.VMEM((1, width), F32),
                pltpu.VMEM((width + tokens, width), BF16),
                pltpu.VMEM((width + tokens, width), BF16),
                pltpu.VMEM((slots, 2, 2, tokens // 2 + width // 4, width), BF16),
                pltpu.VMEM((slots, 2, 2, tokens // 2, width), BF16),
                pltpu.VMEM((rows, width), BF16),
                pltpu.VMEM((rows, width), F32),
                pltpu.VMEM((rows, width), F32),
                pltpu.VMEM((rows, width), F32),
                pltpu.VMEM((width, width), BF16),
                pltpu.VMEM(((chips - chips // 2 + 1) * 2 * tokens, width), BF16),
                pltpu.SemaphoreType.DMA((6,)),
                pltpu.SemaphoreType.DMA((4,)),
                pltpu.SemaphoreType.DMA((4,)),
                pltpu.SemaphoreType.DMA((2, slots)),
                pltpu.SemaphoreType.DMA((2, slots)),
                pltpu.SemaphoreType.DMA((2, slots)),
                pltpu.SemaphoreType.DMA((2, slots)),
                pltpu.SemaphoreType.DMA((2, slots)),
                pltpu.SemaphoreType.DMA((2, slots)),
                pltpu.SemaphoreType.REGULAR((4,)),
            ],
            compiler_params=pltpu.CompilerParams(
                collective_id=0, has_side_effects=True, vmem_limit_bytes=60 * 2**20
            ),
        )(q, k.T, v.T, u.T, beta.T, gain.reshape(1, width))

    return jax.shard_map(
        step,
        mesh=mesh,
        in_specs=(P("seq", "head"),) * 4 + (P("seq", None), P()),
        out_specs=P("seq", "head"),
        check_vma=False,
    )
```
